32 devices in a mesh: dp: 8 (over z, x), shard: 4 (over y, core).
Axes of the slice: x: 2, y: 2, z: 4, core: 2. Of those that a mesh axis runs over, the one named last changes fastest.
Arguments:
- codes: int32 [8, 5, 8, 16], P('dp', None, None, 'shard'), may hold values from 0 to 262143
- lengths: int32 [8], P('dp'), may hold values from 1 to 5, 24 in all
- hidden: bfloat16 [8, 5, 8, 16, 512], P('dp', None, None, 'shard'), may hold values from -6 to 6
- embed: bfloat16 [18, 512], replicated, may hold values from -1.5 to 1.5
- conv_weight: bfloat16 [512, 27, 512], P('shard'), may hold values from -0.0546875 to 0.0546875
- gain: float32 [512], replicated, may hold values from 0.1 to 1.9
- bias: float32 [512], replicated, may hold values from -3 to 3
- cotangent: bfloat16 [8, 5, 16, 32, 128], P('dp', None, None, 'shard'), may hold values from -6 to 6
Outputs:
- decoded: bfloat16 [8, 5, 16, 32, 128], P('dp', None, None, 'shard')
- grad_hidden: bfloat16 [8, 5, 8, 16, 512], P('dp', None, None, 'shard')
- grad_conv: float32 [512, 27, 512], P('shard')
- grad_embed: float32 [18, 512], replicated
- grad_gain: float32 [512], replicated
- grad_bias: float32 [512], replicated
The draws below stay inside these ranges and needn't reach their ends.
Inputs may be any that keep to these rules, and one draw needn't show every extreme that they name: Frames from lengths[c] on are padding; some clip has all 5 frames valid.
All inputs are finite; a program needn't handle non-finite values. No bound on the sum of `lengths` on one device may be relied on, other than what follows from the above.
Results may differ from the reference program's by a relative error of at most 0.02.
Values may be sent and summed in bfloat16 or wider, within the bound.
No kernel may reach another device: no remote copies, remote signals or barrier semaphores. Data moves between devices by JAX's collectives and lax.ppermute only.
A program may use at most 128 MiB of HBM per device.

```python
import math
import jax
import jax.numpy as jnp
import numpy as np
from jax import lax

C = 512
CODE_BITS = 18
GROUPS = 32
FRAMES = 5
ROWS = 8
COLS_DEV = 4
COLS = 16
CLIPS = 8
N_DP = 8
N_SHARD = 4


def with_ends(array, key, least, high):
    index_at = [jax.random.randint(jax.random.fold_in(key, axis), (), 0, length) for axis, length in enumerate(array.shape)]
    main_axis = array.shape.index(max(array.shape))
    next_to = index_at[:main_axis] + [(index_at[main_axis] + 1) % array.shape[main_axis]] + index_at[main_axis + 1:]
    return array.at[tuple(index_at)].set(least).at[tuple(next_to)].set(high)


def shard_levels(key, dims, split, low, top_value):
    loudness = 1.0
    for position, parts in split:
        draws = jax.random.uniform(jax.random.fold_in(jax.random.fold_in(key, 6), position), (parts,), jnp.float32, low / len(split), top_value / len(split))
        loudness = loudness * jnp.repeat(jnp.exp(draws), dims[position] // parts).reshape((-1,) + (1,) * (len(dims) - 1 - position))
    return loudness


def profile(count, total, reach, slope):
    loads = [(1 << 20) // math.isqrt(rank ** slope) + 1 for rank in range(2, count + 1)]
    spare, given = total - reach - (count - 1), [1] * (count - 1)
    while spare > 0:
        free = [i for i in range(count - 1) if given[i] < reach]
        mass, left = sum([loads[i] for i in free]), spare
        for i in free:
            more = min(reach - given[i], max(1, left * loads[i] // mass), spare)
            given[i] = given[i] + more
            spare = spare - more
    return np.array([reach] + given)


def ragged_sizes(stream_key, count, total, limit, slope):
    if count == 2:
        one = jax.random.randint(stream_key, (), max(1, total - limit), min(limit, total - 1) + 1)
        return jnp.stack([one, total - one])
    tallies = jnp.asarray(profile(count, total, limit, slope), jnp.int32)
    couples = (count - 1) // 2
    giver, sink = tallies[1:1 + 2 * couples:2], tallies[2:2 + 2 * couples:2]
    room = jnp.minimum(giver - 1, limit - sink)
    moved = jax.random.randint(jax.random.fold_in(stream_key, 1), (couples,), 0, 1 << 20) % (room + 1)
    tallies = tallies.at[1:1 + 2 * couples:2].set(giver - moved).at[2:2 + 2 * couples:2].set(sink + moved)
    return tallies[jax.random.permutation(jax.random.fold_in(stream_key, 2), count)]


def normal_values(own_key, shape, scale, most, split=(), held_as=jnp.bfloat16):
    level = shard_levels(own_key, shape, split, -0.22, 0.18) if split else 1.0
    drawn = jax.random.normal(own_key, shape, jnp.float32) * scale * level
    return jnp.minimum(jnp.maximum(drawn, -most), most).astype(held_as)


def setup_inputs(seed: int = 0) -> dict:
    streams_of = jax.random.split(jax.random.key(seed), 9)
    return {
        "codes": with_ends(jax.random.randint(streams_of[0], (CLIPS, FRAMES, ROWS, COLS), 0, 262144), jax.random.fold_in(streams_of[0], 1), 0, 262143).astype(jnp.int32),
        "lengths": ragged_sizes(streams_of[1], CLIPS, 3 * N_DP, FRAMES, 0).astype(jnp.int32),
        "hidden": normal_values(streams_of[2], (CLIPS, FRAMES, ROWS, COLS, C), 1.0, 6.0, ((0, 8), (3, 4))),
        "embed": normal_values(streams_of[3], (CODE_BITS, C), CODE_BITS ** -0.5, 1.5),
        "conv_weight": normal_values(streams_of[4], (C, 27, C), (27 * C) ** -0.5, 0.0546875, ((0, 4),)),
        "gain": jnp.clip(1.0 + 0.18 * jax.random.normal(streams_of[5], (C,), jnp.float32), 0.1, 1.9),
        "bias": normal_values(streams_of[6], (C,), 0.5, 3.0, (), jnp.float32),
        "cotangent": normal_values(streams_of[7], (CLIPS, FRAMES, 2 * ROWS, 2 * COLS, C // 4), 1.0, 6.0, ((0, 8), (3, 4))),
    }


def front_patches(padded, frames, height, width):
    taps = []
    for depth_tap in range(3):
        for row_tap in range(3):
            for col_tap in range(3):
                taps.append(padded[depth_tap:depth_tap + frames, row_tap:row_tap + height, col_tap:col_tap + width])
    return jnp.stack(taps, axis=3)

def back_patches(padded, frames, height, width):
    taps = []
    for depth_tap in range(3):
        for row_tap in range(3):
            for col_tap in range(3):
                taps.append(padded[2 - depth_tap:2 - depth_tap + frames, 2 - row_tap:2 - row_tap + height, 2 - col_tap:2 - col_tap + width])
    return jnp.stack(taps, axis=3)

def reference(codes, lengths, hidden, embed, conv_weight, gain, bias, cotangent):
    per_group = C // GROUPS
    quarter = C // 4
    columns = COLS_DEV * N_SHARD
    positions = FRAMES * ROWS * columns
    powers = 2 ** jnp.arange(CODE_BITS, dtype=jnp.int32)
    flat_weight = jnp.transpose(conv_weight, (1, 0, 2)).reshape(27 * C, C)
    back_weight = jnp.transpose(conv_weight, (1, 2, 0)).reshape(27 * C, C)
    gain_group = gain.reshape(GROUPS, per_group)
    bias_group = bias.reshape(GROUPS, per_group)

    def one_clip(carry, inputs):
        total_conv, total_embed, total_gain, total_bias = carry
        clip_codes, clip_length, clip_hidden, clip_cot = inputs
        frame_mask = (jnp.arange(FRAMES) < clip_length).astype(jnp.float32)
        mask_cells = frame_mask[:, None, None, None]
        mask_groups = frame_mask[:, None, None, None, None]
        bits = (clip_codes[..., None] // powers % 2 * 2 - 1).astype(jnp.bfloat16)
        embedded = jnp.dot(bits.reshape(positions, CODE_BITS), embed, preferred_element_type=jnp.float32).reshape(FRAMES, ROWS, columns, C)
        features = ((embedded + clip_hidden.astype(jnp.float32)) * mask_cells).astype(jnp.bfloat16)
        padded = jnp.pad(features, ((2, 0), (1, 1), (1, 1), (0, 0)))
        patches = front_patches(padded, FRAMES, ROWS, columns).reshape(positions, 27 * C)
        conv_out = jnp.dot(patches, flat_weight, preferred_element_type=jnp.float32)
        grouped = conv_out.reshape(FRAMES, ROWS, columns, GROUPS, per_group)
        count = clip_length.astype(jnp.float32) * (ROWS * columns * per_group)
        mean = lax.optimization_barrier(jnp.sum(grouped * mask_groups, axis=(0, 1, 2, 4))) / count
        variance = lax.optimization_barrier(jnp.sum(grouped * grouped * mask_groups, axis=(0, 1, 2, 4))) / count - mean * mean
        inv_std = lax.rsqrt(variance + 1e-05)
        normed = (grouped - mean[:, None]) * inv_std[:, None]
        pre = normed * gain_group + bias_group
        sigma = jax.nn.sigmoid(pre)
        activated = pre * sigma * mask_groups
        decoded = activated.reshape(FRAMES, ROWS, columns, 2, 2, quarter).transpose(0, 1, 3, 2, 4, 5).reshape(FRAMES, 2 * ROWS, 2 * columns, quarter).astype(jnp.bfloat16)
        upstream = clip_cot.astype(jnp.float32).reshape(FRAMES, ROWS, 2, columns, 2, quarter).transpose(0, 1, 3, 2, 4, 5).reshape(FRAMES, ROWS, columns, GROUPS, per_group) * mask_groups
        d_pre = upstream * sigma * (1.0 + pre * (1.0 - sigma))
        gain_term = lax.optimization_barrier(jnp.sum(d_pre * normed, axis=(0, 1, 2))).reshape(C)
        bias_term = lax.optimization_barrier(jnp.sum(d_pre, axis=(0, 1, 2))).reshape(C)
        d_norm = d_pre * gain_group
        tot_one = lax.optimization_barrier(jnp.sum(d_norm, axis=(0, 1, 2, 4)))
        tot_two = lax.optimization_barrier(jnp.sum(d_norm * normed, axis=(0, 1, 2, 4)))
        d_conv = (inv_std[:, None] * (d_norm - tot_one[:, None] / count - normed * tot_two[:, None] / count) * mask_groups).reshape(FRAMES, ROWS, columns, C).astype(jnp.bfloat16)
        grad_padded = jnp.pad(d_conv, ((0, 2), (1, 1), (1, 1), (0, 0)))
        grad_patches = back_patches(grad_padded, FRAMES, ROWS, columns)
        d_features = jnp.dot(grad_patches.reshape(positions, 27 * C), back_weight, preferred_element_type=jnp.float32).astype(jnp.bfloat16).reshape(FRAMES, ROWS, columns, C)
        d_features = d_features * mask_cells.astype(jnp.bfloat16)
        embed_term = jnp.dot(bits.reshape(positions, CODE_BITS).T, d_features.reshape(positions, C), preferred_element_type=jnp.float32)
        clip_sum = jnp.dot(patches.T, d_conv.reshape(positions, C), preferred_element_type=jnp.float32)
        clip_sum = lax.optimization_barrier(clip_sum.astype(jnp.bfloat16)).astype(jnp.float32)
        return ((total_conv + clip_sum, total_embed + embed_term, total_gain + gain_term, total_bias + bias_term), (decoded, d_features))
    init = (jnp.zeros((27 * C, C), jnp.float32), jnp.zeros((CODE_BITS, C), jnp.float32), jnp.zeros((C,), jnp.float32), jnp.zeros((C,), jnp.float32))
    totals, outputs = lax.scan(one_clip, init, (codes, lengths, hidden, cotangent))
    decoded, grad_hidden = outputs
    grad_conv = totals[0].reshape(27, C, C).transpose(1, 0, 2)
    return (decoded, grad_hidden, grad_conv, totals[1], totals[2], totals[3])
```

```python
import jax
import jax.numpy as jnp
from jax import lax
from jax.experimental import pallas as pl
from jax.experimental.pallas import tpu as pltpu
from jax.sharding import PartitionSpec as P

CODE_BITS = 18
GROUPS = 32
LANES = 128
VMEM_BYTES = 56 * 1024 * 1024

eps_norm = 1e-05

bf16 = jnp.bfloat16
f32 = jnp.float32


def kernel_call(body, outs, args, scratch=(), scalars=1, flops=0, aliases=None):
    specs = [pl.BlockSpec(memory_space=pltpu.SMEM)] * scalars
    specs += [pl.BlockSpec(memory_space=pltpu.VMEM)] * (len(args) - scalars)
    moved = sum(a.size * a.dtype.itemsize for a in args)
    moved += sum(o.size * o.dtype.itemsize for o in outs)
    return pl.pallas_call(
        body,
        out_shape=outs,
        in_specs=specs,
        out_specs=[pl.BlockSpec(memory_space=pltpu.VMEM)] * len(outs),
        scratch_shapes=scratch,
        input_output_aliases=aliases or {},
        compiler_params=pltpu.CompilerParams(vmem_limit_bytes=VMEM_BYTES),
        cost_estimate=pl.CostEstimate(flops=flops, bytes_accessed=moved, transcendentals=0),
    )(*args)


def shaped(shape, dtype):
    return jax.ShapeDtypeStruct(shape, dtype)


def swap(block, hop):
    pairs = [(i, i ^ hop) for i in range(lax.axis_size("shard"))]
    return lax.ppermute(block, "shard", pairs)


def step_rows(slab, first, count, step):
    return slab[pl.ds(first, count, stride=step), :]

def frame_rows_below(rows, limit):
    return (lax.broadcasted_iota(jnp.int32, (rows, 1), 0) < limit).astype(f32)


def embed_body(shards, width, frame_rows, info, codes, hidden, embed, cot, *rest):
    sends, (chunks, cot_wide, part) = rest[:shards], rest[shards:]
    rows = codes.shape[0]
    cells = rows // width
    lanes = lax.broadcasted_iota(jnp.int32, (rows, LANES), 1)
    spread = jnp.broadcast_to(codes[...], (rows, LANES))
    bit = lax.bitwise_and(lax.shift_right_logical(spread, jnp.minimum(lanes, 31)), 1)
    bits = jnp.where(lanes < CODE_BITS, 2 * bit - 1, 0).astype(f32).astype(bf16)
    embedded = jnp.dot(bits, embed[...], preferred_element_type=f32)
    mask = frame_rows_below(rows, info[0] * frame_rows)
    features = ((embedded + hidden[...].astype(f32)) * mask).astype(bf16)
    cot_wide[...] = cot[...].astype(f32)
    for j in range(shards):
        chunks[j, :, :LANES] = features[:, j * LANES : (j + 1) * LANES]
        for w in range(width):
            first = (j // 2) * (2 * width) + 2 * w + j % 2
            part[pl.ds(w, cells, stride=width), :] = step_rows(cot_wide, first, cells, 4 * width)
        chunks[j, :, LANES:] = part[...].astype(bf16)
    for hop in range(shards):
        sends[hop][...] = chunks[lax.bitwise_xor(info[1], hop)]


def forward_body(shards, width, frames, height, info, *rest):
    parts, weight = rest[:shards], rest[shards]
    own_out = rest[shards + 1]
    sends = rest[shards + 2 : 2 * shards + 1]
    slab_out, turned_out, cot_out = rest[2 * shards + 1 : 2 * shards + 4]
    chunks, slab, cot, rims, patches, sums = rest[2 * shards + 4 :]
    columns = width * shards
    rows = frames * height * columns
    cells = frames * height
    for hop in range(shards):
        origin = lax.bitwise_xor(info[1], hop)
        chunks[origin, 0] = parts[hop][:, :LANES].astype(f32)
        chunks[origin, 1] = parts[hop][:, LANES:].astype(f32)
    for j in range(shards):
        for w in range(width):
            place = pl.ds(width * j + w, cells, stride=columns)
            slab[place, :] = chunks[j, 0, pl.ds(w, cells, stride=width), :]
            cot[place, :] = chunks[j, 1, pl.ds(w, cells, stride=width), :]
    cot_out[...] = cot[...].astype(bf16)
    middle = slab[...]
    slab_out[...] = middle.astype(bf16)
    turned_out[...] = middle.T.astype(bf16)
    column = lax.broadcasted_iota(jnp.int32, (rows, 1), 0) % columns
    rims[...] = jnp.zeros_like(rims)
    shifted = (
        jnp.where(column > 0, pltpu.roll(middle, 1, 0), 0.0),
        middle,
        jnp.where(column < columns - 1, pltpu.roll(middle, rows - 1, 0), 0.0),
    )
    for dw in range(3):
        rims[dw, 2:, 1 : height + 1] = (
            shifted[dw].astype(bf16).reshape(frames, height, columns, LANES)
        )
    for dt in range(3):
        for dr in range(3):
            for dw in range(3):
                tap = (dt * 3 + dr) * 3 + dw
                patches[:, tap * LANES : (tap + 1) * LANES] = rims[
                    dw, dt : dt + frames, dr : dr + height
                ].reshape(rows, LANES)
    for half in range(shards // 2):
        total = jnp.dot(
            patches[...],
            weight[:, half * 2 * LANES : (half + 1) * 2 * LANES],
            preferred_element_type=f32,
        )
        sums[2 * half] = total[:, :LANES]
        sums[2 * half + 1] = total[:, LANES:]
    own_out[...] = sums[info[1]]
    for hop in range(1, shards):
        sends[hop - 1][...] = sums[lax.bitwise_xor(info[1], hop)].astype(bf16)


def group_total(values, per_group):
    lane = lax.broadcasted_iota(jnp.int32, values.shape, 1)
    step = 1
    while step < per_group:
        above = pltpu.roll(values, LANES - step, 1)
        below = pltpu.roll(values, step, 1)
        values = values + jnp.where(lax.bitwise_and(lane, step) == 0, above, below)
        step *= 2
    return values


def column_total(values):
    return jnp.broadcast_to(jnp.sum(values, axis=0, keepdims=True), (8, LANES))


def norm_body(shards, width, frames, height, per_group, info, *rest):
    own, parts = rest[0], rest[1:shards]
    gain, bias, cot, d_conv_out, terms_out = rest[shards : shards + 5]
    sends = rest[shards + 5 : 2 * shards + 5]
    conv, slope, act, part = rest[2 * shards + 5 :]
    columns = width * shards
    cells = frames * height
    block = height * columns
    length = info[0]
    sum_one = jnp.zeros((8, LANES), f32)
    sum_two = jnp.zeros((8, LANES), f32)
    for t in range(frames):
        span = pl.ds(t * block, block)
        values = own[span, :]
        for received in parts:
            values = values + received[span, :].astype(f32)
        conv[span, :] = values
        mask = (t < length).astype(f32)
        sum_one += column_total(values) * mask
        sum_two += column_total(values * values) * mask
    count = length.astype(f32) * (block * per_group)
    mean = group_total(sum_one, per_group) / count
    variance = group_total(sum_two, per_group) / count - mean * mean
    inv_std = lax.rsqrt(variance + eps_norm)[:1]
    mean = mean[:1]
    gain_sum = jnp.zeros((8, LANES), f32)
    bias_sum = jnp.zeros((8, LANES), f32)
    for t in range(frames):
        span = pl.ds(t * block, block)
        mask = (t < length).astype(f32)
        normed = (conv[span, :] - mean) * inv_std
        pre = normed * gain[...] + bias[...]
        sigma = jax.nn.sigmoid(pre)
        act[span, :] = pre * sigma * mask
        d_pre = cot[span, :].astype(f32) * mask * sigma * (1.0 + pre * (1.0 - sigma))
        conv[span, :] = normed
        slope[span, :] = d_pre
        gain_sum += column_total(d_pre * normed)
        bias_sum += column_total(d_pre)
    row = lax.broadcasted_iota(jnp.int32, (8, LANES), 0)
    terms_out[...] = jnp.where(row == 0, gain_sum, jnp.where(row == 1, bias_sum, 0.0))
    tot_one = (group_total(bias_sum * gain[...], per_group) / count)[:1]
    tot_two = (group_total(gain_sum * gain[...], per_group) / count)[:1]
    for t in range(frames):
        span = pl.ds(t * block, block)
        mask = (t < length).astype(f32)
        d_norm = slope[span, :] * gain[...]
        d_conv_out[span, :] = (
            inv_std * (d_norm - tot_one - conv[span, :] * tot_two) * mask
        ).astype(bf16)
    column_chunks(shards, width, cells, info, act, part, sends)


def column_chunks(shards, width, cells, info, slab, part, sends):
    for j in range(shards):
        for w in range(width):
            part[j, pl.ds(w, cells, stride=width), :] = step_rows(
                slab, width * j + w, cells, width * shards
            )
    for hop in range(shards):
        sends[hop][...] = part[lax.bitwise_xor(info[1], hop)].astype(bf16)


def input_grad_body(shards, width, frames, height, info, *rest):
    parts, weight, codes = rest[:shards], rest[shards], rest[shards + 1 : 2 * shards + 1]
    embed_out = rest[2 * shards + 1]
    sends = rest[2 * shards + 2 : 3 * shards + 2]
    pieces, whole, sums, part = rest[3 * shards + 2 :]
    columns = width * shards
    rows = frames * height * columns
    cells = frames * height
    for hop in range(shards):
        pieces[lax.bitwise_xor(info[1], hop)] = parts[hop][...]
    for j in range(shards):
        whole[:, j * LANES : (j + 1) * LANES] = pieces[j]
    sums[...] = jnp.zeros_like(sums)
    for first in range(0, 27, 2):
        taps = min(2, 27 - first)
        images = lax.dot_general(
            whole[...],
            weight[first * LANES : (first + taps) * LANES, :],
            (((1,), (1,)), ((), ())),
            preferred_element_type=f32,
        )
        for tap in range(first, first + taps):
            dt, dr, dw = tap // 9, tap // 3 % 3, tap % 3
            image = images[:, (tap - first) * LANES : (tap - first + 1) * LANES]
            image = image.reshape(frames, height, columns, LANES)
            low, high = max(0, dr - 1), min(height, height + dr - 1)
            sums[dw, : frames - 2 + dt, low:high] += image[
                2 - dt :, low + 1 - dr : high + 1 - dr
            ]
    column = lax.broadcasted_iota(jnp.int32, (rows, 1), 0) % columns
    after = pltpu.roll(sums[0].reshape(rows, LANES), rows - 1, 0)
    before = pltpu.roll(sums[2].reshape(rows, LANES), 1, 0)
    total = sums[1].reshape(rows, LANES)
    total = total + jnp.where(column < columns - 1, after, 0.0)
    total = total + jnp.where(column > 0, before, 0.0)
    total = total * frame_rows_below(rows, info[0] * (height * columns))
    slab = sums.at[1]
    slab[...] = total.reshape(frames, height, columns, LANES)
    flat = slab.reshape(rows, LANES)
    column_chunks(shards, width, cells, info, flat, part, sends)
    level = lax.broadcasted_iota(jnp.int32, (32, cells * width), 0)
    embed_term = jnp.zeros((32, LANES), f32)
    for hop in range(shards):
        spread = jnp.broadcast_to(codes[hop][...], (32, cells * width))
        bit = lax.bitwise_and(lax.shift_right_logical(spread, level), 1)
        bits = jnp.where(level < CODE_BITS, 2 * bit - 1, 0).astype(f32).astype(bf16)
        embed_term += jnp.dot(bits, sends[hop][...], preferred_element_type=f32)
    embed_out[...] = embed_term


def hidden_body(shards, info, *rest):
    parts, out, pieces = rest[:shards], rest[shards], rest[shards + 1]
    for hop in range(shards):
        pieces[lax.bitwise_xor(info[1], hop)] = parts[hop][...]
    for j in range(shards):
        out[:, j * LANES : (j + 1) * LANES] = pieces[j]


def decoded_body(shards, width, info, *rest):
    parts, out, pieces, slab = rest[:shards], rest[shards], rest[shards + 1], rest[shards + 2]
    cells = parts[0].shape[0] // width
    for hop in range(shards):
        pieces[lax.bitwise_xor(info[1], hop)] = parts[hop][...].astype(f32)
    for j in range(shards):
        for w in range(width):
            first = (j // 2) * (2 * width) + 2 * w + j % 2
            slab[pl.ds(first, cells, stride=4 * width), :] = pieces[
                j, pl.ds(w, cells, stride=width), :
            ]
    out[...] = slab[...].astype(bf16)


def weight_grad_body(frames, height, columns, lengths, turned, grads, out, left, *rights):
    clips = turned.shape[0]
    shards = grads.shape[1]
    block = height * columns
    place = lax.broadcasted_iota(jnp.int32, (1, block), 1)
    row, column = place // columns, place % columns

    def one_clip(clip, base):
        length = lengths[clip]

        def one_frame(t, at):
            here = pl.ds(pl.multiple_of(t * block, block), block)
            there = pl.ds(pl.multiple_of(at * block, block), block)
            image = turned[clip, :, here].astype(f32)
            for dr in range(3):
                for dw in range(3):
                    offset = (dr - 1) * columns + dw - 1
                    moved = pltpu.roll(image, -offset % block, 1) if offset else image
                    if dr == 0:
                        moved = jnp.where(row > 0, moved, 0.0)
                    if dr == 2:
                        moved = jnp.where(row < height - 1, moved, 0.0)
                    if dw == 0:
                        moved = jnp.where(column > 0, moved, 0.0)
                    if dw == 2:
                        moved = jnp.where(column < columns - 1, moved, 0.0)
                    tap = dr * 3 + dw
                    left[tap * LANES : (tap + 1) * LANES, there] = moved.astype(bf16)
            for j in range(shards):
                lanes = slice(j * LANES, (j + 1) * LANES)
                grad = grads[clip, j, here, :]
                rights[2][there, lanes] = grad
                rights[1][there, lanes] = jnp.where(t > 0, grad, jnp.zeros_like(grad))
                rights[0][there, lanes] = jnp.where(t > 1, grad, jnp.zeros_like(grad))
            return at + 1

        return lax.fori_loop(0, length, one_frame, base)

    lax.fori_loop(0, clips, one_clip, 0)
    total = left.shape[1]
    for dt in range(3):
        skip = (2 - dt) * block
        product = jnp.dot(
            left[:, : total - skip], rights[dt][skip:, :], preferred_element_type=f32
        )
        out[dt * 9 : (dt + 1) * 9] = product.reshape(9, LANES, product.shape[1])


def by_slices(codes, lengths, hidden, embed, conv_weight, gain, bias, cotangent):
    _, frames, height, width = codes.shape
    channels = conv_weight.shape[2]
    shards = lax.axis_size("shard")
    clips = lax.axis_size("dp")
    per_group = channels // GROUPS
    columns = width * shards
    cells = frames * height
    rows = cells * columns
    own_rows = cells * width
    block = height * columns
    here = lax.axis_index("shard")
    info = jnp.stack([lengths[0], here.astype(jnp.int32)])
    hops = range(1, shards)
    flat_weight = conv_weight.transpose(1, 0, 2).reshape(27 * LANES, channels)

    chunk = shaped((own_rows, 2 * LANES), bf16)
    sent = kernel_call(
        lambda *refs: embed_body(shards, width, height * width, *refs),
        [chunk] * shards,
        [
            info,
            codes.reshape(own_rows, 1),
            hidden.reshape(own_rows, channels),
            jnp.pad(embed, ((0, LANES - CODE_BITS), (0, 0))),
            cotangent.reshape(rows, LANES),
        ],
        [
            pltpu.VMEM((shards, own_rows, 2 * LANES), bf16),
            pltpu.VMEM((rows, LANES), f32),
            pltpu.VMEM((own_rows, LANES), f32),
        ],
        flops=2 * own_rows * LANES * channels,
    )
    code_row = codes.reshape(1, own_rows)
    all_codes = [code_row] + [swap(code_row, hop) for hop in hops]
    parts = [sent[0]] + [swap(sent[hop], hop) for hop in hops]

    slab = shaped((rows, LANES), bf16)
    forward = kernel_call(
        lambda *refs: forward_body(shards, width, frames, height, *refs),
        [shaped((rows, LANES), f32)] + [slab] * (shards - 1)
        + [slab, shaped((LANES, rows), bf16), slab],
        [info, *parts, flat_weight],
        [
            pltpu.VMEM((shards, 2, own_rows, LANES), f32),
            pltpu.VMEM((rows, LANES), f32),
            pltpu.VMEM((rows, LANES), f32),
            pltpu.VMEM((3, frames + 2, height + 2, columns, LANES), bf16),
            pltpu.VMEM((rows, 27 * LANES), bf16),
            pltpu.VMEM((shards, rows, LANES), f32),
        ],
        flops=2 * rows * 27 * LANES * channels,
    )
    own_sum, sum_sends = forward[0], forward[1:shards]
    turned, cot_slab = forward[shards + 1], forward[shards + 2]
    all_turned = lax.all_gather(turned, "dp", axis=0)
    all_lengths = lax.all_gather(lengths, "dp", axis=0, tiled=True)
    sum_parts = [swap(sum_sends[hop - 1], hop) for hop in hops]

    small = shaped((own_rows, LANES), bf16)
    normed = kernel_call(
        lambda *refs: norm_body(shards, width, frames, height, per_group, *refs),
        [slab, shaped((8, LANES), f32)] + [small] * shards,
        [
            info,
            own_sum,
            *sum_parts,
            lax.dynamic_slice_in_dim(gain, here * LANES, LANES).reshape(1, LANES),
            lax.dynamic_slice_in_dim(bias, here * LANES, LANES).reshape(1, LANES),
            cot_slab,
        ],
        [pltpu.VMEM((rows, LANES), f32)] * 3 + [pltpu.VMEM((shards, own_rows, LANES), f32)],
        flops=rows * LANES * 40,
    )
    d_conv, terms, act_sends = normed[0], normed[1], normed[2:]
    d_parts = [d_conv] + [swap(d_conv, hop) for hop in hops]
    all_grads = lax.all_gather(d_conv, ("dp", "shard"), axis=0).reshape(
        clips, shards, rows, LANES
    )
    act_parts = [act_sends[0]] + [swap(act_sends[hop], hop) for hop in hops]

    back = kernel_call(
        lambda *refs: input_grad_body(shards, width, frames, height, *refs),
        [shaped((32, LANES), f32)] + [small] * shards,
        [info, *d_parts, flat_weight, *all_codes],
        [
            pltpu.VMEM((shards, rows, LANES), bf16),
            pltpu.VMEM((rows, channels), bf16),
            pltpu.VMEM((3, frames, height, columns, LANES), f32),
            pltpu.VMEM((shards, own_rows, LANES), f32),
        ],
        flops=2 * rows * 27 * LANES * channels,
    )
    embed_term, hidden_sends = back[0], back[1:]
    hidden_parts = [hidden_sends[0]] + [swap(hidden_sends[hop], hop) for hop in hops]
    grad_hidden = kernel_call(
        lambda *refs: hidden_body(shards, *refs),
        [shaped((own_rows, channels), bf16)],
        [info, *hidden_parts],
        [pltpu.VMEM((shards, own_rows, LANES), bf16)],
    )[0]
    decoded = kernel_call(
        lambda *refs: decoded_body(shards, width, *refs),
        [slab],
        [info, *act_parts],
        [pltpu.VMEM((shards, own_rows, LANES), f32), pltpu.VMEM((rows, LANES), f32)],
    )[0]
    valid = 3 * clips * block
    grad_weight = kernel_call(
        lambda *refs: weight_grad_body(frames, height, columns, *refs),
        [shaped((27, LANES, channels), f32)],
        [all_lengths, all_turned, all_grads],
        [pltpu.VMEM((9 * LANES, valid), bf16)] + [pltpu.VMEM((valid, channels), bf16)] * 3,
        flops=2 * valid * 27 * LANES * channels,
    )[0]
    grad_conv = grad_weight.transpose(1, 0, 2)

    small_sum = lax.psum(jnp.concatenate([embed_term, terms], axis=0), "dp")
    all_small = lax.all_gather(small_sum, "shard", axis=1, tiled=True)
    return (
        decoded.reshape(1, frames, 2 * height, 2 * width, LANES),
        grad_hidden.reshape(1, frames, height, width, channels),
        grad_conv,
        all_small[:CODE_BITS],
        all_small[32],
        all_small[33],
    )


def extended(block, sides, width):
    for axis, dim in sides:
        count = lax.axis_size(axis)
        forward = [(i, i + 1) for i in range(count - 1)]
        backward = [(target, source) for source, target in forward]
        low = lax.ppermute(
            lax.slice_in_dim(block, block.shape[dim] - width, None, axis=dim), axis, forward
        )
        high = lax.ppermute(lax.slice_in_dim(block, 0, width, axis=dim), axis, backward)
        block = jnp.concatenate([low, block, high], axis=dim)
    return block


def forward_taps(padded, frames, height, width):
    taps = []
    for depth_tap in range(3):
        for row_tap in range(3):
            for col_tap in range(3):
                taps.append(
                    padded[
                        depth_tap : depth_tap + frames,
                        row_tap : row_tap + height,
                        col_tap : col_tap + width,
                    ]
                )
    return taps


def backward_taps(padded, frames, height, width):
    taps = []
    for depth_tap in range(3):
        for row_tap in range(3):
            for col_tap in range(3):
                taps.append(
                    padded[
                        2 - depth_tap : 2 - depth_tap + frames,
                        2 - row_tap : 2 - row_tap + height,
                        2 - col_tap : 2 - col_tap + width,
                    ]
                )
    return taps


def own_columns(rimmed, frames, height, width):
    padded = jnp.pad(rimmed, ((2, 0), (1, 1), (0, 0), (0, 0)))
    return jnp.stack(forward_taps(padded, frames, height, width), axis=3)


def slab_columns(spread, frames, height, slab_width):
    padded = jnp.pad(spread, ((2, 0), (1, 1), (1, 1), (0, 0)))
    return jnp.concatenate(forward_taps(padded, frames, height, slab_width), axis=3)


def by_gathers(codes, lengths, hidden, embed, conv_weight, gain, bias, cotangent):
    frames = codes.shape[1]
    height = codes.shape[2]
    width = codes.shape[3]
    share = conv_weight.shape[0]
    channels = conv_weight.shape[2]
    quarter = channels // 4
    shards = lax.axis_size("shard")
    slab_width = width * shards
    positions = frames * height * width
    groups = GROUPS
    per_group = channels // groups
    frame_mask = (jnp.arange(frames) < lengths[0]).astype(jnp.float32)
    mask_cells = frame_mask[:, None, None, None]
    mask_groups = frame_mask[:, None, None, None, None]
    powers = 2 ** jnp.arange(CODE_BITS, dtype=jnp.int32)
    bits = (codes[0][..., None] // powers % 2 * 2 - 1).astype(jnp.bfloat16)
    embedded = jnp.dot(
        bits.reshape(positions, CODE_BITS), embed, preferred_element_type=jnp.float32
    ).reshape(frames, height, width, channels)
    features = ((embedded + hidden[0].astype(jnp.float32)) * mask_cells).astype(jnp.bfloat16)
    rimmed = extended(features, (("shard", 2),), 1)
    own_patches = own_columns(rimmed, frames, height, width)
    conv_out = jnp.einsum(
        "frwtn,ntc->frwc",
        own_patches,
        lax.all_gather(conv_weight, "shard", axis=0, tiled=True),
        preferred_element_type=jnp.float32,
    )
    grouped = conv_out.reshape(frames, height, width, groups, per_group)
    sum_one, sum_two = lax.psum(
        (
            jnp.sum(grouped * mask_groups, axis=(0, 1, 2, 4)),
            jnp.sum(grouped * grouped * mask_groups, axis=(0, 1, 2, 4)),
        ),
        "shard",
    )
    count = lengths[0].astype(jnp.float32) * (height * width * shards * per_group)
    mean = sum_one / count
    variance = sum_two / count - mean * mean
    inv_std = lax.rsqrt(variance + eps_norm)
    gain_group = gain.reshape(groups, per_group)
    bias_group = bias.reshape(groups, per_group)
    normed = (grouped - mean[:, None]) * inv_std[:, None]
    pre = normed * gain_group + bias_group
    sigma = jax.nn.sigmoid(pre)
    activated = pre * sigma * mask_groups
    decoded = (
        activated.reshape(frames, height, width, 2, 2, quarter)
        .transpose(0, 1, 3, 2, 4, 5)
        .reshape(frames, 2 * height, 2 * width, quarter)
        .astype(jnp.bfloat16)[None]
    )
    upstream = (
        cotangent[0]
        .astype(jnp.float32)
        .reshape(frames, height, 2, width, 2, quarter)
        .transpose(0, 1, 3, 2, 4, 5)
        .reshape(frames, height, width, groups, per_group)
        * mask_groups
    )
    d_pre = upstream * sigma * (1.0 + pre * (1.0 - sigma))
    gain_term = jnp.sum(d_pre * normed, axis=(0, 1, 2)).reshape(channels)
    bias_term = jnp.sum(d_pre, axis=(0, 1, 2)).reshape(channels)
    d_norm = d_pre * gain_group
    tot_one, tot_two = lax.psum(
        (jnp.sum(d_norm, axis=(0, 1, 2, 4)), jnp.sum(d_norm * normed, axis=(0, 1, 2, 4))), "shard"
    )
    d_conv = (
        (
            inv_std[:, None]
            * (d_norm - tot_one[:, None] / count - normed * tot_two[:, None] / count)
            * mask_groups
        )
        .reshape(frames, height, width, channels)
        .astype(jnp.bfloat16)
    )
    spread_back = lax.all_to_all(features, "shard", split_axis=3, concat_axis=2, tiled=True)
    slab_back = slab_columns(spread_back, frames, height, slab_width)
    whole_grad = lax.all_gather(d_conv, "shard", axis=2, tiled=True)
    back_share = jnp.transpose(conv_weight, (2, 1, 0)).reshape(channels, 27 * share)
    tap_images = jnp.dot(
        whole_grad.reshape(-1, channels), back_share, preferred_element_type=jnp.float32
    ).reshape(frames, height, slab_width, 27 * share)
    padded_images = jnp.pad(tap_images, ((0, 2), (1, 1), (1, 1), (0, 0)))
    input_sum = jnp.zeros((frames, height, slab_width, share), jnp.float32)
    for tap_index, shifted in enumerate(backward_taps(padded_images, frames, height, slab_width)):
        input_sum = input_sum + shifted[..., tap_index * share : (tap_index + 1) * share]
    d_features = lax.all_to_all(
        input_sum.astype(jnp.bfloat16), "shard", split_axis=2, concat_axis=3, tiled=True
    )
    clip_part = jnp.einsum(
        "pk,pc->kc",
        slab_back.reshape(-1, 27 * share),
        whole_grad.reshape(-1, channels),
        preferred_element_type=jnp.float32,
    )
    weight_sum = clip_part.reshape(27, share, channels).transpose(1, 0, 2)
    grad_conv = lax.psum(weight_sum.astype(jnp.bfloat16), "dp").astype(jnp.float32)
    grad_hidden = d_features * mask_cells.astype(jnp.bfloat16)
    embed_term = jnp.dot(
        bits.reshape(positions, CODE_BITS).T,
        grad_hidden.reshape(positions, channels),
        preferred_element_type=jnp.float32,
    )
    grad_embed, grad_gain, grad_bias = lax.psum((embed_term, gain_term, bias_term), ("dp", "shard"))
    return (decoded, grad_hidden[None], grad_conv, grad_embed, grad_gain, grad_bias)


def on_device(codes, lengths, hidden, embed, conv_weight, gain, bias, cotangent):
    share = conv_weight.shape[0]
    block = codes.shape[2] * codes.shape[3] * lax.axis_size("shard")
    plan = by_slices if share == LANES and block == LANES else by_gathers
    return plan(codes, lengths, hidden, embed, conv_weight, gain, bias, cotangent)


def solution(mesh):
    return jax.shard_map(
        on_device,
        mesh=mesh,
        in_specs=(
            P("dp", None, None, "shard"),
            P("dp"),
            P("dp", None, None, "shard", None),
            P(),
            P("shard", None, None),
            P(),
            P(),
            P("dp", None, None, "shard", None),
        ),
        out_specs=(
            P("dp", None, None, "shard", None),
            P("dp", None, None, "shard", None),
            P("shard", None, None),
            P(),
            P(),
            P(),
        ),
        check_vma=False,
    )
```

```python
import jax
import jax.numpy as jnp
from jax import lax
from jax.experimental import pallas as pl
from jax.experimental.pallas import tpu as pltpu
from jax.sharding import PartitionSpec as P

CODE_BITS = 18
GROUPS = 32
LANES = 128
LENGTH_ROWS = 16
VMEM_BYTES = 56 * 1024 * 1024

eps_norm = 1e-05

bf16 = jnp.bfloat16
f32 = jnp.float32


def kernel_call(body, outs, args, scratch=(), scalars=1, flops=0, aliases=None):
    specs = [pl.BlockSpec(memory_space=pltpu.SMEM)] * scalars
    specs += [pl.BlockSpec(memory_space=pltpu.VMEM)] * (len(args) - scalars)
    moved = sum(a.size * a.dtype.itemsize for a in args)
    moved += sum(o.size * o.dtype.itemsize for o in outs)
    return pl.pallas_call(
        body,
        out_shape=outs,
        in_specs=specs,
        out_specs=[pl.BlockSpec(memory_space=pltpu.VMEM)] * len(outs),
        scratch_shapes=scratch,
        input_output_aliases=aliases or {},
        compiler_params=pltpu.CompilerParams(vmem_limit_bytes=VMEM_BYTES),
        cost_estimate=pl.CostEstimate(flops=flops, bytes_accessed=moved, transcendentals=0),
    )(*args)


def shaped(shape, dtype):
    return jax.ShapeDtypeStruct(shape, dtype)


def swap(block, hop):
    pairs = [(i, i ^ hop) for i in range(lax.axis_size("shard"))]
    return lax.ppermute(block, "shard", pairs)


def step_rows(slab, first, count, step):
    return slab[pl.ds(first, count, stride=step), :]

def frame_rows_below(rows, limit):
    return (lax.broadcasted_iota(jnp.int32, (rows, 1), 0) < limit).astype(f32)


def embed_body(shards, width, frame_rows, info, codes, hidden, embed, cot, *rest):
    sends, (chunks, cot_wide, part) = rest[:shards], rest[shards:]
    rows = codes.shape[0]
    cells = rows // width
    lanes = lax.broadcasted_iota(jnp.int32, (rows, LANES), 1)
    spread = jnp.broadcast_to(codes[...], (rows, LANES))
    bit = lax.bitwise_and(lax.shift_right_logical(spread, jnp.minimum(lanes, 31)), 1)
    bits = jnp.where(lanes < CODE_BITS, 2 * bit - 1, 0).astype(f32).astype(bf16)
    embedded = jnp.dot(bits, embed[...], preferred_element_type=f32)
    mask = frame_rows_below(rows, info[0] * frame_rows)
    features = ((embedded + hidden[...].astype(f32)) * mask).astype(bf16)
    cot_wide[...] = cot[...].astype(f32)
    for j in range(shards):
        chunks[j, :, :LANES] = features[:, j * LANES : (j + 1) * LANES]
        for w in range(width):
            first = (j // 2) * (2 * width) + 2 * w + j % 2
            part[pl.ds(w, cells, stride=width), :] = step_rows(cot_wide, first, cells, 4 * width)
        chunks[j, :, LANES:] = part[...].astype(bf16)
    for hop in range(shards):
        sends[hop][...] = chunks[lax.bitwise_xor(info[1], hop)]


def forward_body(shards, width, frames, height, info, *rest):
    parts, weight = rest[:shards], rest[shards]
    own_out = rest[shards + 1]
    sends = rest[shards + 2 : 2 * shards + 1]
    slab_out, turned_out, cot_out = rest[2 * shards + 1 : 2 * shards + 4]
    chunks, slab, cot, rims, patches, sums = rest[2 * shards + 4 :]
    columns = width * shards
    rows = frames * height * columns
    cells = frames * height
    for hop in range(shards):
        origin = lax.bitwise_xor(info[1], hop)
        chunks[origin, 0] = parts[hop][:, :LANES].astype(f32)
        chunks[origin, 1] = parts[hop][:, LANES:].astype(f32)
    for j in range(shards):
        for w in range(width):
            place = pl.ds(width * j + w, cells, stride=columns)
            slab[place, :] = chunks[j, 0, pl.ds(w, cells, stride=width), :]
            cot[place, :] = chunks[j, 1, pl.ds(w, cells, stride=width), :]
    cot_out[...] = cot[...].astype(bf16)
    middle = slab[...]
    slab_out[...] = middle.astype(bf16)
    turned_out[:LANES, :] = middle.T.astype(bf16)
    turned_out[LANES:, :] = jnp.full((LENGTH_ROWS, rows), info[0].astype(f32)).astype(bf16)
    column = lax.broadcasted_iota(jnp.int32, (rows, 1), 0) % columns
    rims[...] = jnp.zeros_like(rims)
    shifted = (
        jnp.where(column > 0, pltpu.roll(middle, 1, 0), 0.0),
        middle,
        jnp.where(column < columns - 1, pltpu.roll(middle, rows - 1, 0), 0.0),
    )
    for dw in range(3):
        rims[dw, 2:, 1 : height + 1] = (
            shifted[dw].astype(bf16).reshape(frames, height, columns, LANES)
        )
    for dt in range(3):
        for dr in range(3):
            for dw in range(3):
                tap = (dt * 3 + dr) * 3 + dw
                patches[:, tap * LANES : (tap + 1) * LANES] = rims[
                    dw, dt : dt + frames, dr : dr + height
                ].reshape(rows, LANES)
    for half in range(shards // 2):
        total = jnp.dot(
            patches[...],
            weight[:, half * 2 * LANES : (half + 1) * 2 * LANES],
            preferred_element_type=f32,
        )
        sums[2 * half] = total[:, :LANES]
        sums[2 * half + 1] = total[:, LANES:]
    own_out[...] = sums[info[1]]
    for hop in range(1, shards):
        sends[hop - 1][...] = sums[lax.bitwise_xor(info[1], hop)].astype(bf16)


def group_total(values, per_group):
    lane = lax.broadcasted_iota(jnp.int32, values.shape, 1)
    step = 1
    while step < per_group:
        above = pltpu.roll(values, LANES - step, 1)
        below = pltpu.roll(values, step, 1)
        values = values + jnp.where(lax.bitwise_and(lane, step) == 0, above, below)
        step *= 2
    return values


def column_total(values):
    return jnp.broadcast_to(jnp.sum(values, axis=0, keepdims=True), (8, LANES))


def norm_body(shards, width, frames, height, per_group, info, *rest):
    own, parts = rest[0], rest[1:shards]
    gain, bias, cot, d_conv_out, terms_out = rest[shards : shards + 5]
    sends = rest[shards + 5 : 2 * shards + 5]
    conv, slope, act, part = rest[2 * shards + 5 :]
    columns = width * shards
    cells = frames * height
    block = height * columns
    length = info[0]
    sum_one = jnp.zeros((8, LANES), f32)
    sum_two = jnp.zeros((8, LANES), f32)
    for t in range(frames):
        span = pl.ds(t * block, block)
        values = own[span, :]
        for received in parts:
            values = values + received[span, :].astype(f32)
        conv[span, :] = values
        mask = (t < length).astype(f32)
        sum_one += column_total(values) * mask
        sum_two += column_total(values * values) * mask
    count = length.astype(f32) * (block * per_group)
    mean = group_total(sum_one, per_group) / count
    variance = group_total(sum_two, per_group) / count - mean * mean
    inv_std = lax.rsqrt(variance + eps_norm)[:1]
    mean = mean[:1]
    gain_sum = jnp.zeros((8, LANES), f32)
    bias_sum = jnp.zeros((8, LANES), f32)
    for t in range(frames):
        span = pl.ds(t * block, block)
        mask = (t < length).astype(f32)
        normed = (conv[span, :] - mean) * inv_std
        pre = normed * gain[...] + bias[...]
        sigma = jax.nn.sigmoid(pre)
        act[span, :] = pre * sigma * mask
        d_pre = cot[span, :].astype(f32) * mask * sigma * (1.0 + pre * (1.0 - sigma))
        conv[span, :] = normed
        slope[span, :] = d_pre
        gain_sum += column_total(d_pre * normed)
        bias_sum += column_total(d_pre)
    row = lax.broadcasted_iota(jnp.int32, (8, LANES), 0)
    terms_out[...] = jnp.where(row == 0, gain_sum, jnp.where(row == 1, bias_sum, 0.0))
    tot_one = (group_total(bias_sum * gain[...], per_group) / count)[:1]
    tot_two = (group_total(gain_sum * gain[...], per_group) / count)[:1]
    for t in range(frames):
        span = pl.ds(t * block, block)
        mask = (t < length).astype(f32)
        d_norm = slope[span, :] * gain[...]
        d_conv_out[span, :] = (
            inv_std * (d_norm - tot_one - conv[span, :] * tot_two) * mask
        ).astype(bf16)
    column_chunks(shards, width, cells, info, act, part, sends)


def column_chunks(shards, width, cells, info, slab, part, sends):
    for j in range(shards):
        for w in range(width):
            part[j, pl.ds(w, cells, stride=width), :] = step_rows(
                slab, width * j + w, cells, width * shards
            )
    for hop in range(shards):
        sends[hop][...] = part[lax.bitwise_xor(info[1], hop)].astype(bf16)


def input_grad_body(shards, width, frames, height, info, *rest):
    parts, weight, codes = rest[:shards], rest[shards], rest[shards + 1 : 2 * shards + 1]
    embed_out = rest[2 * shards + 1]
    sends = rest[2 * shards + 2 : 3 * shards + 2]
    pieces, whole, sums, part = rest[3 * shards + 2 :]
    columns = width * shards
    rows = frames * height * columns
    cells = frames * height
    for hop in range(shards):
        pieces[lax.bitwise_xor(info[1], hop)] = parts[hop][...]
    for j in range(shards):
        whole[:, j * LANES : (j + 1) * LANES] = pieces[j]
    sums[...] = jnp.zeros_like(sums)
    for first in range(0, 27, 2):
        taps = min(2, 27 - first)
        images = lax.dot_general(
            whole[...],
            weight[first * LANES : (first + taps) * LANES, :],
            (((1,), (1,)), ((), ())),
            preferred_element_type=f32,
        )
        for tap in range(first, first + taps):
            dt, dr, dw = tap // 9, tap // 3 % 3, tap % 3
            image = images[:, (tap - first) * LANES : (tap - first + 1) * LANES]
            image = image.reshape(frames, height, columns, LANES)
            low, high = max(0, dr - 1), min(height, height + dr - 1)
            sums[dw, : frames - 2 + dt, low:high] += image[
                2 - dt :, low + 1 - dr : high + 1 - dr
            ]
    column = lax.broadcasted_iota(jnp.int32, (rows, 1), 0) % columns
    after = pltpu.roll(sums[0].reshape(rows, LANES), rows - 1, 0)
    before = pltpu.roll(sums[2].reshape(rows, LANES), 1, 0)
    total = sums[1].reshape(rows, LANES)
    total = total + jnp.where(column < columns - 1, after, 0.0)
    total = total + jnp.where(column > 0, before, 0.0)
    total = total * frame_rows_below(rows, info[0] * (height * columns))
    slab = sums.at[1]
    slab[...] = total.reshape(frames, height, columns, LANES)
    flat = slab.reshape(rows, LANES)
    column_chunks(shards, width, cells, info, flat, part, sends)
    level = lax.broadcasted_iota(jnp.int32, (32, cells * width), 0)
    embed_term = jnp.zeros((32, LANES), f32)
    for hop in range(shards):
        spread = jnp.broadcast_to(codes[hop][...], (32, cells * width))
        bit = lax.bitwise_and(lax.shift_right_logical(spread, level), 1)
        bits = jnp.where(level < CODE_BITS, 2 * bit - 1, 0).astype(f32).astype(bf16)
        embed_term += jnp.dot(bits, sends[hop][...], preferred_element_type=f32)
    embed_out[...] = embed_term


def hidden_body(shards, info, *rest):
    parts, out, pieces = rest[:shards], rest[shards], rest[shards + 1]
    for hop in range(shards):
        pieces[lax.bitwise_xor(info[1], hop)] = parts[hop][...]
    for j in range(shards):
        out[:, j * LANES : (j + 1) * LANES] = pieces[j]


def decoded_body(shards, width, info, *rest):
    parts, out, pieces, slab = rest[:shards], rest[shards], rest[shards + 1], rest[shards + 2]
    cells = parts[0].shape[0] // width
    for hop in range(shards):
        pieces[lax.bitwise_xor(info[1], hop)] = parts[hop][...].astype(f32)
    for j in range(shards):
        for w in range(width):
            first = (j // 2) * (2 * width) + 2 * w + j % 2
            slab[pl.ds(first, cells, stride=4 * width), :] = pieces[
                j, pl.ds(w, cells, stride=width), :
            ]
    out[...] = slab[...].astype(bf16)


def terms_body(shards, info, *rest):
    parts, (embed_out, gain_out, bias_out) = rest[:shards], rest[shards : shards + 3]
    pieces = rest[shards + 3]
    for hop in range(shards):
        pieces[lax.bitwise_xor(info[1], hop)] = parts[hop][...]
    for j in range(shards):
        lanes = slice(j * LANES, (j + 1) * LANES)
        embed_out[:, lanes] = pieces[j, :CODE_BITS]
        gain_out[:, lanes] = pieces[j, 32:33]
        bias_out[:, lanes] = pieces[j, 33:34]


def weight_grad_body(frames, height, columns, labels, info, turned, *rest):
    grads, out = rest[: len(labels)], rest[len(labels)]
    left, right_two, right_one, right_now, starts = rest[len(labels) + 1 :]
    clips = turned.shape[0]
    block = height * columns
    place = lax.broadcasted_iota(jnp.int32, (1, block), 1)
    row, column = place // columns, place % columns

    start = jnp.int32(0)
    for clip in range(clips):
        starts[clip] = start
        length = jnp.max(turned[clip, LANES:, :LANES].astype(f32)).astype(jnp.int32)
        start = start + length
    starts[clips] = start

    def one_clip(clip, _):
        base = starts[clip]

        def one_frame(t, _):
            here = pl.ds(pl.multiple_of(t * block, block), block)
            there = pl.ds(pl.multiple_of((base + t) * block, block), block)
            image = turned[clip, :LANES, here].astype(f32)
            for dr in range(3):
                for dw in range(3):
                    offset = (dr - 1) * columns + dw - 1
                    moved = pltpu.roll(image, -offset % block, 1) if offset else image
                    if dr == 0:
                        moved = jnp.where(row > 0, moved, 0.0)
                    if dr == 2:
                        moved = jnp.where(row < height - 1, moved, 0.0)
                    if dw == 0:
                        moved = jnp.where(column > 0, moved, 0.0)
                    if dw == 2:
                        moved = jnp.where(column < columns - 1, moved, 0.0)
                    tap = dr * 3 + dw
                    left[tap * LANES : (tap + 1) * LANES, there] = moved.astype(bf16)
            return 0

        return lax.fori_loop(0, starts[clip + 1] - base, one_frame, 0)

    lax.fori_loop(0, clips, one_clip, 0)
    for grad, label in zip(grads, labels):
        clip, part = piece_origin(info, label, clips)
        base = starts[clip]
        lanes = pl.ds(pl.multiple_of(part * LANES, LANES), LANES)

        def one_piece(t, _, grad=grad, base=base, lanes=lanes):
            here = pl.ds(pl.multiple_of(t * block, block), block)
            there = pl.ds(pl.multiple_of((base + t) * block, block), block)
            image = grad[here, :]
            right_now[there, lanes] = image
            right_one[there, lanes] = jnp.where(t > 0, image, jnp.zeros_like(image))
            right_two[there, lanes] = jnp.where(t > 1, image, jnp.zeros_like(image))
            return 0

        lax.fori_loop(0, starts[clip + 1] - base, one_piece, 0)
    total = left.shape[1]
    for dt, right in enumerate((right_two, right_one, right_now)):
        skip = (2 - dt) * block
        product = jnp.dot(
            left[:, : total - skip], right[skip:, :], preferred_element_type=f32
        )
        out[dt * 9 : (dt + 1) * 9] = product.reshape(9, LANES, product.shape[1])


def piece_origin(info, label, clips):
    kind, hop, partner = label
    mine = lax.bitwise_xor(info[1], partner)
    core = lax.bitwise_and(mine, 1)
    line = lax.rem(info[2] // 2 + clips // 2 - hop, clips // 2)
    side = lax.rem(info[2], 2)
    if kind == 0:
        other_clip, other_part = 0, 0
    elif kind == 3:
        other_clip, other_part = 1, 2
    elif hop == 0:
        other_clip, other_part = (1, 0) if kind == 1 else (0, 2)
    elif kind == 1:
        other_clip, other_part = 1 - core, 2 * core
    else:
        other_clip, other_part = core, 2 * (1 - core)
    return 2 * line + lax.bitwise_xor(side, other_clip), lax.bitwise_xor(mine, other_part)


def send(block, target):
    lines, shards = lax.axis_size("dp") // 2, lax.axis_size("shard")
    pairs = []
    for line in range(lines):
        for side in range(2):
            for chip in range(shards // 2):
                for core in range(2):
                    to_line, to_side, to_chip, to_core = target(line, side, chip, core)
                    source = (line * 2 + side) * shards + chip * 2 + core
                    sink = (to_line % lines * 2 + to_side) * shards + to_chip * 2 + to_core
                    pairs.append((source, sink))
    return lax.ppermute(block, ("dp", "shard"), pairs)


def to_side(line, side, chip, core):
    return line, 1 - side, chip, core


def to_chip(line, side, chip, core):
    return line, side, 1 - chip, core


def to_core(line, side, chip, core):
    return line, side, chip, 1 - core


def to_side_or_chip(line, side, chip, core):
    return (line, 1 - side, chip, core) if core == 0 else (line, side, 1 - chip, core)


def to_chip_or_side(line, side, chip, core):
    return (line, 1 - side, chip, core) if core == 1 else (line, side, 1 - chip, core)


def spread_over_clips(own, other_chip):
    lines = lax.axis_size("dp") // 2
    core_zero = lax.axis_index("shard") % 2 == 0
    held, labels = [], []
    same = [own]
    for hop in range(1, lines):
        same.append(send(own, lambda l, s, c, k, hop=hop: (l + hop, s, c, k)))
    first = [send(own, to_side)]
    first += [send(same[hop], to_side_or_chip) for hop in range(1, lines)]
    second = [other_chip]
    second += [send(same[hop], to_chip_or_side) for hop in range(1, lines)]
    third = [send(jnp.where(core_zero, first[0], other_chip), to_chip_or_side)]
    third += [send(first[hop], to_chip_or_side) for hop in range(1, lines)]
    for hop in range(lines):
        for kind, group in enumerate((same, first, second, third)):
            held.append(group[hop])
            labels.append((kind, hop, 0))
            if hop or kind in (1, 3):
                held.append(send(group[hop], to_core))
                labels.append((kind, hop, 1))
    return held, labels


def by_slices(codes, lengths, hidden, embed, conv_weight, gain, bias, cotangent):
    _, frames, height, width = codes.shape
    channels = conv_weight.shape[2]
    shards = lax.axis_size("shard")
    clips = lax.axis_size("dp")
    per_group = channels // GROUPS
    columns = width * shards
    cells = frames * height
    rows = cells * columns
    own_rows = cells * width
    block = height * columns
    here = lax.axis_index("shard")
    info = jnp.stack([lengths[0], here, lax.axis_index("dp")])
    hops = range(1, shards)
    flat_weight = conv_weight.transpose(1, 0, 2).reshape(27 * LANES, channels)

    chunk = shaped((own_rows, 2 * LANES), bf16)
    sent = kernel_call(
        lambda *refs: embed_body(shards, width, height * width, *refs),
        [chunk] * shards,
        [
            info,
            codes.reshape(own_rows, 1),
            hidden.reshape(own_rows, channels),
            jnp.pad(embed, ((0, LANES - CODE_BITS), (0, 0))),
            cotangent.reshape(rows, LANES),
        ],
        [
            pltpu.VMEM((shards, own_rows, 2 * LANES), bf16),
            pltpu.VMEM((rows, LANES), f32),
            pltpu.VMEM((own_rows, LANES), f32),
        ],
        flops=2 * own_rows * LANES * channels,
    )
    code_row = codes.reshape(1, own_rows)
    all_codes = [code_row] + [swap(code_row, hop) for hop in hops]
    parts = [sent[0]] + [swap(sent[hop], hop) for hop in hops]

    slab = shaped((rows, LANES), bf16)
    forward = kernel_call(
        lambda *refs: forward_body(shards, width, frames, height, *refs),
        [shaped((rows, LANES), f32)] + [slab] * (shards - 1)
        + [slab, shaped((LANES + LENGTH_ROWS, rows), bf16), slab],
        [info, *parts, flat_weight],
        [
            pltpu.VMEM((shards, 2, own_rows, LANES), f32),
            pltpu.VMEM((rows, LANES), f32),
            pltpu.VMEM((rows, LANES), f32),
            pltpu.VMEM((3, frames + 2, height + 2, columns, LANES), bf16),
            pltpu.VMEM((rows, 27 * LANES), bf16),
            pltpu.VMEM((shards, rows, LANES), f32),
        ],
        flops=2 * rows * 27 * LANES * channels,
    )
    own_sum, sum_sends = forward[0], forward[1:shards]
    turned, cot_slab = forward[shards + 1], forward[shards + 2]
    all_turned = lax.all_gather(turned, "dp", axis=0)
    sum_parts = [swap(sum_sends[hop - 1], hop) for hop in hops]

    small = shaped((own_rows, LANES), bf16)
    normed = kernel_call(
        lambda *refs: norm_body(shards, width, frames, height, per_group, *refs),
        [slab, shaped((8, LANES), f32)] + [small] * shards,
        [
            info,
            own_sum,
            *sum_parts,
            lax.dynamic_slice_in_dim(gain, here * LANES, LANES).reshape(1, LANES),
            lax.dynamic_slice_in_dim(bias, here * LANES, LANES).reshape(1, LANES),
            cot_slab,
        ],
        [pltpu.VMEM((rows, LANES), f32)] * 3 + [pltpu.VMEM((shards, own_rows, LANES), f32)],
        flops=rows * LANES * 40,
    )
    d_conv, terms, act_sends = normed[0], normed[1], normed[2:]
    far = swap(d_conv, 2)
    d_parts = [d_conv, swap(d_conv, 1), far, swap(far, 1)]
    grads, labels = spread_over_clips(d_conv, far)
    grads += [d_parts[1], d_parts[3]]
    labels += [(0, 0, 1), (2, 0, 1)]
    act_parts = [act_sends[0]] + [swap(act_sends[hop], hop) for hop in hops]

    back = kernel_call(
        lambda *refs: input_grad_body(shards, width, frames, height, *refs),
        [shaped((32, LANES), f32)] + [small] * shards,
        [info, *d_parts, flat_weight, *all_codes],
        [
            pltpu.VMEM((shards, rows, LANES), bf16),
            pltpu.VMEM((rows, channels), bf16),
            pltpu.VMEM((3, frames, height, columns, LANES), f32),
            pltpu.VMEM((shards, own_rows, LANES), f32),
        ],
        flops=2 * rows * 27 * LANES * channels,
    )
    embed_term, hidden_sends = back[0], back[1:]
    hidden_parts = [hidden_sends[0]] + [swap(hidden_sends[hop], hop) for hop in hops]
    grad_hidden = kernel_call(
        lambda *refs: hidden_body(shards, *refs),
        [shaped((own_rows, channels), bf16)],
        [info, *hidden_parts],
        [pltpu.VMEM((shards, own_rows, LANES), bf16)],
    )[0]
    decoded = kernel_call(
        lambda *refs: decoded_body(shards, width, *refs),
        [slab],
        [info, *act_parts],
        [pltpu.VMEM((shards, own_rows, LANES), f32), pltpu.VMEM((rows, LANES), f32)],
    )[0]
    valid = 3 * clips * block
    grad_weight = kernel_call(
        lambda *refs: weight_grad_body(frames, height, columns, labels, *refs),
        [shaped((27, LANES, channels), f32)],
        [info, all_turned, *grads],
        [pltpu.VMEM((9 * LANES, valid), bf16)]
        + [pltpu.VMEM((valid, channels), bf16)] * 3
        + [pltpu.SMEM((clips + 1,), jnp.int32)],
        flops=2 * valid * 27 * LANES * channels,
    )[0]
    grad_conv = grad_weight.transpose(1, 0, 2)

    term = jnp.concatenate([embed_term, terms], axis=0)
    hop = 1
    while hop < clips:
        term = term + lax.ppermute(term, "dp", [(i, i ^ hop) for i in range(clips)])
        hop *= 2
    term_parts = [term] + [swap(term, hop) for hop in hops]
    grad_embed, grad_gain, grad_bias = kernel_call(
        lambda *refs: terms_body(shards, *refs),
        [shaped((CODE_BITS, channels), f32)] + [shaped((1, channels), f32)] * 2,
        [info, *term_parts],
        [pltpu.VMEM((shards, 40, LANES), f32)],
    )
    return (
        decoded.reshape(1, frames, 2 * height, 2 * width, LANES),
        grad_hidden.reshape(1, frames, height, width, channels),
        grad_conv,
        grad_embed,
        grad_gain.reshape(channels),
        grad_bias.reshape(channels),
    )


def extended(block, sides, width):
    for axis, dim in sides:
        count = lax.axis_size(axis)
        forward = [(i, i + 1) for i in range(count - 1)]
        backward = [(target, source) for source, target in forward]
        low = lax.ppermute(
            lax.slice_in_dim(block, block.shape[dim] - width, None, axis=dim), axis, forward
        )
        high = lax.ppermute(lax.slice_in_dim(block, 0, width, axis=dim), axis, backward)
        block = jnp.concatenate([low, block, high], axis=dim)
    return block


def forward_taps(padded, frames, height, width):
    taps = []
    for depth_tap in range(3):
        for row_tap in range(3):
            for col_tap in range(3):
                taps.append(
                    padded[
                        depth_tap : depth_tap + frames,
                        row_tap : row_tap + height,
                        col_tap : col_tap + width,
                    ]
                )
    return taps


def backward_taps(padded, frames, height, width):
    taps = []
    for depth_tap in range(3):
        for row_tap in range(3):
            for col_tap in range(3):
                taps.append(
                    padded[
                        2 - depth_tap : 2 - depth_tap + frames,
                        2 - row_tap : 2 - row_tap + height,
                        2 - col_tap : 2 - col_tap + width,
                    ]
                )
    return taps


def own_columns(rimmed, frames, height, width):
    padded = jnp.pad(rimmed, ((2, 0), (1, 1), (0, 0), (0, 0)))
    return jnp.stack(forward_taps(padded, frames, height, width), axis=3)


def slab_columns(spread, frames, height, slab_width):
    padded = jnp.pad(spread, ((2, 0), (1, 1), (1, 1), (0, 0)))
    return jnp.concatenate(forward_taps(padded, frames, height, slab_width), axis=3)


def by_gathers(codes, lengths, hidden, embed, conv_weight, gain, bias, cotangent):
    frames = codes.shape[1]
    height = codes.shape[2]
    width = codes.shape[3]
    share = conv_weight.shape[0]
    channels = conv_weight.shape[2]
    quarter = channels // 4
    shards = lax.axis_size("shard")
    slab_width = width * shards
    positions = frames * height * width
    groups = GROUPS
    per_group = channels // groups
    frame_mask = (jnp.arange(frames) < lengths[0]).astype(jnp.float32)
    mask_cells = frame_mask[:, None, None, None]
    mask_groups = frame_mask[:, None, None, None, None]
    powers = 2 ** jnp.arange(CODE_BITS, dtype=jnp.int32)
    bits = (codes[0][..., None] // powers % 2 * 2 - 1).astype(jnp.bfloat16)
    embedded = jnp.dot(
        bits.reshape(positions, CODE_BITS), embed, preferred_element_type=jnp.float32
    ).reshape(frames, height, width, channels)
    features = ((embedded + hidden[0].astype(jnp.float32)) * mask_cells).astype(jnp.bfloat16)
    rimmed = extended(features, (("shard", 2),), 1)
    own_patches = own_columns(rimmed, frames, height, width)
    conv_out = jnp.einsum(
        "frwtn,ntc->frwc",
        own_patches,
        lax.all_gather(conv_weight, "shard", axis=0, tiled=True),
        preferred_element_type=jnp.float32,
    )
    grouped = conv_out.reshape(frames, height, width, groups, per_group)
    sum_one, sum_two = lax.psum(
        (
            jnp.sum(grouped * mask_groups, axis=(0, 1, 2, 4)),
            jnp.sum(grouped * grouped * mask_groups, axis=(0, 1, 2, 4)),
        ),
        "shard",
    )
    count = lengths[0].astype(jnp.float32) * (height * width * shards * per_group)
    mean = sum_one / count
    variance = sum_two / count - mean * mean
    inv_std = lax.rsqrt(variance + eps_norm)
    gain_group = gain.reshape(groups, per_group)
    bias_group = bias.reshape(groups, per_group)
    normed = (grouped - mean[:, None]) * inv_std[:, None]
    pre = normed * gain_group + bias_group
    sigma = jax.nn.sigmoid(pre)
    activated = pre * sigma * mask_groups
    decoded = (
        activated.reshape(frames, height, width, 2, 2, quarter)
        .transpose(0, 1, 3, 2, 4, 5)
        .reshape(frames, 2 * height, 2 * width, quarter)
        .astype(jnp.bfloat16)[None]
    )
    upstream = (
        cotangent[0]
        .astype(jnp.float32)
        .reshape(frames, height, 2, width, 2, quarter)
        .transpose(0, 1, 3, 2, 4, 5)
        .reshape(frames, height, width, groups, per_group)
        * mask_groups
    )
    d_pre = upstream * sigma * (1.0 + pre * (1.0 - sigma))
    gain_term = jnp.sum(d_pre * normed, axis=(0, 1, 2)).reshape(channels)
    bias_term = jnp.sum(d_pre, axis=(0, 1, 2)).reshape(channels)
    d_norm = d_pre * gain_group
    tot_one, tot_two = lax.psum(
        (jnp.sum(d_norm, axis=(0, 1, 2, 4)), jnp.sum(d_norm * normed, axis=(0, 1, 2, 4))), "shard"
    )
    d_conv = (
        (
            inv_std[:, None]
            * (d_norm - tot_one[:, None] / count - normed * tot_two[:, None] / count)
            * mask_groups
        )
        .reshape(frames, height, width, channels)
        .astype(jnp.bfloat16)
    )
    spread_back = lax.all_to_all(features, "shard", split_axis=3, concat_axis=2, tiled=True)
    slab_back = slab_columns(spread_back, frames, height, slab_width)
    whole_grad = lax.all_gather(d_conv, "shard", axis=2, tiled=True)
    back_share = jnp.transpose(conv_weight, (2, 1, 0)).reshape(channels, 27 * share)
    tap_images = jnp.dot(
        whole_grad.reshape(-1, channels), back_share, preferred_element_type=jnp.float32
    ).reshape(frames, height, slab_width, 27 * share)
    padded_images = jnp.pad(tap_images, ((0, 2), (1, 1), (1, 1), (0, 0)))
    input_sum = jnp.zeros((frames, height, slab_width, share), jnp.float32)
    for tap_index, shifted in enumerate(backward_taps(padded_images, frames, height, slab_width)):
        input_sum = input_sum + shifted[..., tap_index * share : (tap_index + 1) * share]
    d_features = lax.all_to_all(
        input_sum.astype(jnp.bfloat16), "shard", split_axis=2, concat_axis=3, tiled=True
    )
    clip_part = jnp.einsum(
        "pk,pc->kc",
        slab_back.reshape(-1, 27 * share),
        whole_grad.reshape(-1, channels),
        preferred_element_type=jnp.float32,
    )
    weight_sum = clip_part.reshape(27, share, channels).transpose(1, 0, 2)
    grad_conv = lax.psum(weight_sum.astype(jnp.bfloat16), "dp").astype(jnp.float32)
    grad_hidden = d_features * mask_cells.astype(jnp.bfloat16)
    embed_term = jnp.dot(
        bits.reshape(positions, CODE_BITS).T,
        grad_hidden.reshape(positions, channels),
        preferred_element_type=jnp.float32,
    )
    grad_embed, grad_gain, grad_bias = lax.psum((embed_term, gain_term, bias_term), ("dp", "shard"))
    return (decoded, grad_hidden[None], grad_conv, grad_embed, grad_gain, grad_bias)


def on_device(codes, lengths, hidden, embed, conv_weight, gain, bias, cotangent):
    share = conv_weight.shape[0]
    block = codes.shape[2] * codes.shape[3] * lax.axis_size("shard")
    fits = share == LANES and block == LANES and lax.axis_size("shard") == 4
    plan = by_slices if fits and lax.axis_size("dp") == 8 else by_gathers
    return plan(codes, lengths, hidden, embed, conv_weight, gain, bias, cotangent)


def solution(mesh):
    return jax.shard_map(
        on_device,
        mesh=mesh,
        in_specs=(
            P("dp", None, None, "shard"),
            P("dp"),
            P("dp", None, None, "shard", None),
            P(),
            P("shard", None, None),
            P(),
            P(),
            P("dp", None, None, "shard", None),
        ),
        out_specs=(
            P("dp", None, None, "shard", None),
            P("dp", None, None, "shard", None),
            P("shard", None, None),
            P(),
            P(),
            P(),
        ),
        check_vma=False,
    )
```

```python
import math

import jax
import jax.numpy as jnp
from jax import lax
from jax.experimental import pallas as pl
from jax.experimental.pallas import tpu as pltpu
from jax.sharding import PartitionSpec as P

CODE_BITS = 18
GROUPS = 32
LANES = 128
LENGTH_ROWS = 16
BIT_ROWS = 32
TERM_ROW = 24
MIB = 1024 * 1024
WIDE_LIMIT = 61 * MIB
SMALL_COST = pl.CostEstimate(flops=1, bytes_accessed=1, transcendentals=0)

eps_norm = 1e-05

bf16 = jnp.bfloat16
f32 = jnp.float32


def scratch_bytes(scratch):
    held = [s for s in scratch if s.dtype in (bf16, f32)]
    return sum(math.prod(s.shape) * jnp.dtype(s.dtype).itemsize for s in held)


def kernel_call(body, outs, args, scratch=(), scalars=1, flops=0, anywhere=()):
    vmem = pl.BlockSpec(memory_space=pltpu.VMEM)
    specs = [pl.BlockSpec(memory_space=pltpu.SMEM)] * scalars
    specs += [vmem] * (len(args) - scalars)
    for place in anywhere:
        specs[place] = pl.BlockSpec(memory_space=pltpu.HBM)
    moved = sum(a.size * a.dtype.itemsize for a in args)
    moved += sum(o.size * o.dtype.itemsize for o in outs)
    limit = min(56 * MIB, moved + scratch_bytes(scratch) + 12 * MIB)
    if anywhere:
        limit = WIDE_LIMIT
    return pl.pallas_call(
        body,
        out_shape=outs,
        in_specs=specs,
        out_specs=[vmem] * len(outs),
        scratch_shapes=scratch,
        compiler_params=pltpu.CompilerParams(vmem_limit_bytes=limit),
        cost_estimate=SMALL_COST,
    )(*args)


def shaped(shape, dtype):
    return jax.ShapeDtypeStruct(shape, dtype)


def swap(block, hop):
    pairs = [(i, i ^ hop) for i in range(lax.axis_size("shard"))]
    return lax.ppermute(block, "shard", pairs)


def step_rows(slab, first, count, step):
    return slab[pl.ds(first, count, stride=step), :]

def frame_rows_below(rows, limit):
    return (lax.broadcasted_iota(jnp.int32, (rows, 1), 0) < limit).astype(f32)


def embed_body(shards, width, frame_rows, info, codes, hidden, embed, cot, *rest):
    sends, (chunks, cot_wide, part, table) = rest[:shards], rest[shards:]
    rows = codes.shape[0]
    cells = rows // width
    lanes = lax.broadcasted_iota(jnp.int32, (rows, LANES), 1)
    spread = jnp.broadcast_to(codes[...], (rows, LANES))
    bit = lax.bitwise_and(lax.shift_right_logical(spread, jnp.minimum(lanes, 31)), 1)
    bits = jnp.where(lanes < CODE_BITS, 2 * bit - 1, 0).astype(f32)
    turned_bits = jnp.concatenate(
        [bits.T[:BIT_ROWS], jnp.zeros((BIT_ROWS, 2 * LANES - rows), f32)], axis=1
    ).astype(bf16)
    bits = bits.astype(bf16)
    table[...] = jnp.zeros_like(table)
    table[:CODE_BITS, :] = embed[...]
    embedded = jnp.dot(bits, table[...], preferred_element_type=f32)
    mask = frame_rows_below(rows, info[0] * frame_rows)
    features = ((embedded + hidden[...].astype(f32)) * mask).astype(bf16)
    cot_wide[...] = cot[...].astype(f32)
    for j in range(shards):
        chunks[j, :rows, :LANES] = features[:, j * LANES : (j + 1) * LANES]
        for w in range(width):
            first = (j // 2) * (2 * width) + 2 * w + j % 2
            part[pl.ds(w, cells, stride=width), :] = step_rows(cot_wide, first, cells, 4 * width)
        chunks[j, :rows, LANES:] = part[...].astype(bf16)
        chunks[j, rows:, :] = turned_bits
    for hop in range(shards):
        sends[hop][...] = chunks[lax.bitwise_xor(info[1], hop)]


def slab_body(shards, width, cells, info, *rest):
    parts, (slab_out, turned_out, cot_out) = rest[:shards], rest[shards : shards + 3]
    chunks, slab, cot = rest[shards + 3 :]
    columns = width * shards
    for hop in range(shards):
        origin = lax.bitwise_xor(info[1], hop)
        chunks[origin, 0] = parts[hop][: cells * width, :LANES].astype(f32)
        chunks[origin, 1] = parts[hop][: cells * width, LANES:].astype(f32)
    for j in range(shards):
        for w in range(width):
            place = pl.ds(width * j + w, cells, stride=columns)
            slab[place, :] = chunks[j, 0, pl.ds(w, cells, stride=width), :]
            cot[place, :] = chunks[j, 1, pl.ds(w, cells, stride=width), :]
    cot_out[...] = cot[...].astype(bf16)
    slab_out[...] = slab[...].astype(bf16)
    turned_out[:LANES, :] = slab[...].T.astype(bf16)
    rows = cells * columns
    turned_out[LANES:, :] = jnp.full((LENGTH_ROWS, rows), info[0].astype(f32)).astype(bf16)


def forward_body(shards, width, frames, height, info, slab, weight, own_out, *rest):
    sends, (rims, patches, sums, held, sems) = rest[: shards - 1], rest[shards - 1 :]
    span = 9 * LANES
    copies = []
    for dt in range(3):
        chunk = pl.ds(dt * span, span)
        copies.append(pltpu.make_async_copy(weight.at[chunk], held.at[chunk], sems.at[dt]))
        copies[dt].start()
    columns = width * shards
    rows = frames * height * columns
    middle = slab[...].astype(f32)
    column = lax.broadcasted_iota(jnp.int32, (rows, 1), 0) % columns
    rims[...] = jnp.zeros_like(rims)
    shifted = (
        jnp.where(column > 0, pltpu.roll(middle, 1, 0), 0.0),
        middle,
        jnp.where(column < columns - 1, pltpu.roll(middle, rows - 1, 0), 0.0),
    )
    for dw in range(3):
        rims[dw, 2:, 1 : height + 1] = (
            shifted[dw].astype(bf16).reshape(frames, height, columns, LANES)
        )
    for dt in range(3):
        for dr in range(3):
            for dw in range(3):
                tap = (dt * 3 + dr) * 3 + dw
                patches[:, tap * LANES : (tap + 1) * LANES] = rims[
                    dw, dt : dt + frames, dr : dr + height
                ].reshape(rows, LANES)
    for dt in range(3):
        copies[dt].wait()
        chunk = slice(dt * span, (dt + 1) * span)
        total = jnp.dot(patches[:, chunk], held[chunk, :], preferred_element_type=f32)
        for part in range(shards):
            piece = total[:, part * LANES : (part + 1) * LANES]
            if dt == 0:
                sums[part] = piece
            else:
                sums[part] += piece
    own_out[...] = sums[info[1]]
    for hop in range(1, shards):
        sends[hop - 1][...] = sums[lax.bitwise_xor(info[1], hop)].astype(bf16)


def group_total(values, per_group):
    lane = lax.broadcasted_iota(jnp.int32, values.shape, 1)
    step = 1
    while step < per_group:
        above = pltpu.roll(values, LANES - step, 1)
        below = pltpu.roll(values, step, 1)
        values = values + jnp.where(lax.bitwise_and(lane, step) == 0, above, below)
        step *= 2
    return values


def column_total(values):
    return jnp.broadcast_to(jnp.sum(values, axis=0, keepdims=True), (8, LANES))


def norm_body(shards, width, frames, height, per_group, info, *rest):
    own, parts = rest[0], rest[1:shards]
    gain_all, bias_all, cot, d_conv_out, terms_out, act = rest[shards : shards + 6]
    conv, slope, scale, sems = rest[shards + 6 :]
    own_lanes = pl.ds(pl.multiple_of(info[1] * LANES, LANES), LANES)
    copies = []
    for place, source in enumerate((gain_all, bias_all)):
        copies.append(pltpu.make_async_copy(source, scale.at[place], sems.at[place]))
        copies[place].start()
    columns = width * shards
    block = height * columns
    length = info[0]
    sum_one = jnp.zeros((8, LANES), f32)
    sum_two = jnp.zeros((8, LANES), f32)
    for t in range(frames):
        span = pl.ds(t * block, block)
        values = own[span, :]
        for received in parts:
            values = values + received[span, :].astype(f32)
        conv[span, :] = values
        mask = (t < length).astype(f32)
        sum_one += column_total(values) * mask
        sum_two += column_total(values * values) * mask
    count = length.astype(f32) * (block * per_group)
    mean = group_total(sum_one, per_group) / count
    variance = group_total(sum_two, per_group) / count - mean * mean
    inv_std = lax.rsqrt(variance + eps_norm)[:1]
    mean = mean[:1]
    for copy in copies:
        copy.wait()
    gain, bias = scale[0, :, own_lanes], scale[1, :, own_lanes]
    gain_sum = jnp.zeros((8, LANES), f32)
    bias_sum = jnp.zeros((8, LANES), f32)
    for t in range(frames):
        span = pl.ds(t * block, block)
        mask = (t < length).astype(f32)
        normed = (conv[span, :] - mean) * inv_std
        pre = normed * gain + bias
        sigma = jax.nn.sigmoid(pre)
        act[span, :] = (pre * sigma * mask).astype(bf16)
        d_pre = cot[span, :].astype(f32) * mask * sigma * (1.0 + pre * (1.0 - sigma))
        conv[span, :] = normed
        slope[span, :] = d_pre
        gain_sum += column_total(d_pre * normed)
        bias_sum += column_total(d_pre)
    row = lax.broadcasted_iota(jnp.int32, (8, LANES), 0)
    terms_out[...] = jnp.where(row == 0, gain_sum, jnp.where(row == 1, bias_sum, 0.0))
    tot_one = (group_total(bias_sum * gain, per_group) / count)[:1]
    tot_two = (group_total(gain_sum * gain, per_group) / count)[:1]
    for t in range(frames):
        span = pl.ds(t * block, block)
        mask = (t < length).astype(f32)
        d_norm = slope[span, :] * gain
        d_conv_out[span, :] = (
            inv_std * (d_norm - tot_one - conv[span, :] * tot_two) * mask
        ).astype(bf16)


def column_chunks(shards, width, cells, slab, part):
    for j in range(shards):
        for w in range(width):
            part[j, pl.ds(w, cells, stride=width), :] = step_rows(
                slab, width * j + w, cells, width * shards
            )


def input_grad_body(shards, width, frames, height, info, *rest):
    own, near, mixed = rest[0], rest[1], rest[2:6]
    weight, act, terms = rest[6:9]
    parts = rest[9 : 9 + shards]
    small_out = rest[9 + shards]
    sends = rest[10 + shards : 10 + 2 * shards]
    whole, sums, slab, part, wide = rest[10 + 2 * shards :]
    columns = width * shards
    rows = frames * height * columns
    cells = frames * height
    own_rows = cells * width
    core = lax.bitwise_and(info[1], 1)

    def place(piece, hop, when):
        @pl.when(when)
        def _():
            origin = lax.bitwise_xor(info[1], hop)
            lanes = pl.ds(pl.multiple_of(origin * LANES, LANES), LANES)
            whole[:, lanes] = piece[...]

    always = info[1] >= 0
    place(own, 0, always)
    place(near, 1, always)
    place(mixed[0], 2, core == 1)
    place(mixed[1], 2, core == 0)
    place(mixed[2], 3, core == 0)
    place(mixed[3], 3, core == 1)
    sums[...] = jnp.zeros_like(sums)
    for first in range(0, 27, 2):
        taps = min(2, 27 - first)
        images = lax.dot_general(
            whole[...],
            weight[first * LANES : (first + taps) * LANES, :],
            (((1,), (1,)), ((), ())),
            preferred_element_type=f32,
        )
        for tap in range(first, first + taps):
            dt, dr, dw = tap // 9, tap // 3 % 3, tap % 3
            image = images[:, (tap - first) * LANES : (tap - first + 1) * LANES]
            image = image.reshape(frames, height, columns, LANES)
            low, high = max(0, dr - 1), min(height, height + dr - 1)
            sums[dw, : frames - 2 + dt, low:high] += image[
                2 - dt :, low + 1 - dr : high + 1 - dr
            ]
    column = lax.broadcasted_iota(jnp.int32, (rows, 1), 0) % columns
    after = pltpu.roll(sums[0].reshape(rows, LANES), rows - 1, 0)
    before = pltpu.roll(sums[2].reshape(rows, LANES), 1, 0)
    total = sums[1].reshape(rows, LANES)
    total = total + jnp.where(column < columns - 1, after, 0.0)
    total = total + jnp.where(column > 0, before, 0.0)
    slab[...] = total * frame_rows_below(rows, info[0] * (height * columns))
    wide[...] = act[...].astype(f32)
    small = jnp.zeros((BIT_ROWS, LANES), f32)
    column_chunks(shards, width, cells, slab, part)
    for hop in range(shards):
        grad = part[lax.bitwise_xor(info[1], hop)].astype(bf16)
        sends[hop][:, :LANES] = grad
        bits = parts[hop][own_rows:, :own_rows]
        small += jnp.dot(bits, grad, preferred_element_type=f32)
    column_chunks(shards, width, cells, wide, part)
    for hop in range(shards):
        sends[hop][:, LANES:] = part[lax.bitwise_xor(info[1], hop)].astype(bf16)
    small_out[:TERM_ROW, :] = small[:TERM_ROW]
    small_out[TERM_ROW:, :] = terms[...]


def finish_body(shards, width, info, *rest):
    parts, (hidden_out, decoded_out, active, slab) = rest[:shards], rest[shards:]
    cells = parts[0].shape[0] // width
    for hop in range(shards):
        origin = lax.bitwise_xor(info[1], hop)
        lanes = pl.ds(pl.multiple_of(origin * LANES, LANES), LANES)
        hidden_out[:, lanes] = parts[hop][:, :LANES]
        active[origin] = parts[hop][:, LANES:].astype(f32)
    for j in range(shards):
        for w in range(width):
            first = (j // 2) * (2 * width) + 2 * w + j % 2
            slab[pl.ds(first, cells, stride=4 * width), :] = active[
                j, pl.ds(w, cells, stride=width), :
            ]
    decoded_out[...] = slab[...].astype(bf16)


def terms_body(shards, info, *rest):
    parts, (embed_out, gain_out, bias_out) = rest[:shards], rest[shards:]
    for hop in range(shards):
        origin = lax.bitwise_xor(info[1], hop)
        lanes = pl.ds(pl.multiple_of(origin * LANES, LANES), LANES)
        embed_out[:, lanes] = parts[hop][:CODE_BITS, :]
        gain_out[:, lanes] = parts[hop][TERM_ROW : TERM_ROW + 1, :]
        bias_out[:, lanes] = parts[hop][TERM_ROW + 1 : TERM_ROW + 2, :]


def slot_clip(info, slot, clips):
    lines = clips // 2
    line = lax.rem(info[2] // 2 + lines - slot % lines, lines)
    return 2 * line + lax.bitwise_xor(lax.rem(info[2], 2), slot // lines)


def by_hop(group):
    own, odd, even = group
    return [own, odd.at[0], even, odd.at[1]]


def fill_taps(frames, height, columns, info, groups, left, table, images, shifts):
    turned = by_hop(groups[:3]) + by_hop(groups[3:])
    clips = len(turned)
    block = height * columns
    source = lax.broadcasted_iota(jnp.int32, (block, block), 0)
    place = lax.broadcasted_iota(jnp.int32, (block, block), 1)
    row, column = place // columns, place % columns
    for dr in range(3):
        for dw in range(3):
            tap = dr * 3 + dw
            match = source == place + (dr - 1) * columns + dw - 1
            if dr == 0:
                match = jnp.logical_and(match, row > 0)
            if dr == 2:
                match = jnp.logical_and(match, row < height - 1)
            if dw == 0:
                match = jnp.logical_and(match, column > 0)
            if dw == 2:
                match = jnp.logical_and(match, column < columns - 1)
            shifts[:, tap * block : (tap + 1) * block] = match.astype(f32).astype(bf16)

    for slot in range(clips):
        length = jnp.max(turned[slot][LANES:, :LANES].astype(f32)).astype(jnp.int32)
        table[slot_clip(info, slot, clips)] = length
    early = jnp.int32(0)
    for clip in range(clips):
        early = early + jnp.maximum(table[clip] - 2, 0)
    first, middle = jnp.int32(0), early
    for clip in range(clips):
        length = table[clip]
        for t in range(frames):
            left_over = length - 1 - t
            at = jnp.where(left_over == 1, middle, first + t)
            table[clips + clip * frames + t] = jnp.where(left_over == 0, 2 * clips + clip, at)
        first = first + jnp.maximum(length - 2, 0)
        middle = middle + jnp.minimum(length - 1, 1)

    for slot in range(clips):
        clip = slot_clip(info, slot, clips)
        for t in range(frames):

            @pl.when(t < table[clip])
            def _(slot=slot, clip=clip, t=t):
                at = table[clips + clip * frames + t]
                there = pl.ds(pl.multiple_of(at * LANES, LANES), LANES)
                images[there, :] = turned[slot][:LANES, t * block : (t + 1) * block]

    step = 4
    for n in range(0, 3 * clips, step):
        moved = jnp.dot(
            images[n * LANES : (n + step) * LANES, :], shifts[...], preferred_element_type=f32
        ).astype(bf16)
        for frame in range(step):
            lanes = slice((n + frame) * block, (n + frame + 1) * block)
            for tap in range(9):
                left[tap * LANES : (tap + 1) * LANES, lanes] = moved[
                    frame * LANES : (frame + 1) * LANES, tap * block : (tap + 1) * block
                ]


def weight_grad_body(frames, height, columns, clips, info, *rest):
    groups, pieces, out = rest[:6], rest[6:30], rest[30]
    rights, (product, left, table, images, shifts, near, line) = rest[31:34], rest[34:41]
    in_sems, sems = rest[41:]
    block = height * columns
    fetches = []
    for kind in range(8):
        targets = near.at[kind], line.at[kind, pl.ds(0, 2)], line.at[kind, 2]
        for place, target in enumerate(targets):
            source = pieces[3 * kind + place]
            fetches.append(pltpu.make_async_copy(source, target, in_sems.at[3 * kind + place]))
            fetches[-1].start()
    fill_taps(frames, height, columns, info, groups, left, table, images, shifts)
    for fetch in fetches:
        fetch.wait()
    held = []
    for kind in range(8):
        held.append([near.at[kind], line.at[kind, 0], line.at[kind, 2], line.at[kind, 1]])
    lines = clips // 2
    core = lax.bitwise_and(info[1], 1)
    rights[2][clips * block :, :] = jnp.zeros_like(rights[2][clips * block :, :])

    def place(slot, t, mine):
        found = []
        for hop in range(2):
            same, side, chip, cross = (held[4 * hop + kind][slot % lines] for kind in range(4))
            if hop != mine:
                side, chip = chip, side
            found += [(hop, same), (hop + 2, chip)] if slot < lines else [
                (hop, side), (hop + 2, cross)
            ]
        clip = slot_clip(info, slot, clips)
        for hop, image in found:
            part = lax.bitwise_xor(info[1], hop)
            lanes = pl.ds(pl.multiple_of(part * LANES, LANES), LANES)
            value = image[t * block : (t + 1) * block, :]
            for lag in range(min(t + 1, 3)):
                at = table[clips + clip * frames + t - lag]
                there = pl.ds(pl.multiple_of(at * block, block), block)
                rights[lag][there, lanes] = value

    for mine in range(2):

        @pl.when(core == mine)
        def _(mine=mine):
            for slot in range(clips):
                for t in range(frames):

                    @pl.when(t < table[slot_clip(info, slot, clips)])
                    def _(slot=slot, t=t):
                        place(slot, t, mine)

    copies = []
    for lag in range(3):
        used = rights[lag].shape[0]
        product[2 - lag] = jnp.dot(
            left[:, :used], rights[lag][...], preferred_element_type=f32
        ).reshape(9, LANES, rights[lag].shape[1])
        copy = pltpu.make_async_copy(
            product.at[2 - lag], out.at[pl.ds((2 - lag) * 9, 9)], sems.at[lag]
        )
        copy.start()
        copies.append(copy)
    for copy in copies:
        copy.wait()


def pack(blocks):
    def body(*refs):
        for place, ref in enumerate(refs[:-1]):
            refs[-1][place] = ref[...]

    vmem = pl.BlockSpec(memory_space=pltpu.VMEM)
    size = len(blocks) * blocks[0].size
    return pl.pallas_call(
        body,
        out_shape=shaped((len(blocks), *blocks[0].shape), blocks[0].dtype),
        in_specs=[vmem] * len(blocks),
        out_specs=vmem,
        compiler_params=pltpu.CompilerParams(vmem_limit_bytes=4 * MIB),
        cost_estimate=SMALL_COST,
    )(*blocks)


def send(block, target):
    lines, shards = lax.axis_size("dp") // 2, lax.axis_size("shard")
    pairs = []
    for line in range(lines):
        for side in range(2):
            for chip in range(shards // 2):
                for core in range(2):
                    to_line, to_side, to_chip, to_core = target(line, side, chip, core)
                    source = (line * 2 + side) * shards + chip * 2 + core
                    sink = (to_line % lines * 2 + to_side) * shards + to_chip * 2 + to_core
                    pairs.append((source, sink))
    return lax.ppermute(block, ("dp", "shard"), pairs)


def to_side(line, side, chip, core):
    return line, 1 - side, chip, core


def to_chip(line, side, chip, core):
    return line, side, 1 - chip, core


def to_core(line, side, chip, core):
    return line, side, chip, 1 - core


def to_side_or_chip(line, side, chip, core):
    return (line, 1 - side, chip, core) if core == 0 else (line, side, 1 - chip, core)


def to_chip_or_side(line, side, chip, core):
    return (line, 1 - side, chip, core) if core == 1 else (line, side, 1 - chip, core)


def fence(*values):
    return lax.optimization_barrier(values)


def by_slices(codes, lengths, hidden, embed, conv_weight, gain, bias, cotangent):
    _, frames, height, width = codes.shape
    channels = conv_weight.shape[2]
    shards = lax.axis_size("shard")
    clips = lax.axis_size("dp")
    per_group = channels // GROUPS
    columns = width * shards
    cells = frames * height
    rows = cells * columns
    own_rows = cells * width
    block = height * columns
    here = lax.axis_index("shard")
    info = jnp.stack([lengths[0], here, lax.axis_index("dp")])
    hops = range(1, shards)
    flat_weight = conv_weight.transpose(1, 0, 2).reshape(27 * LANES, channels)

    chunk = shaped((own_rows + BIT_ROWS, 2 * LANES), bf16)
    sent = kernel_call(
        lambda *refs: embed_body(shards, width, height * width, *refs),
        [chunk] * shards,
        [
            info,
            codes.reshape(own_rows, 1),
            hidden.reshape(own_rows, channels),
            embed,
            cotangent.reshape(rows, LANES),
        ],
        [
            pltpu.VMEM((shards, own_rows + BIT_ROWS, 2 * LANES), bf16),
            pltpu.VMEM((rows, LANES), f32),
            pltpu.VMEM((own_rows, LANES), f32),
            pltpu.VMEM((LANES, channels), bf16),
        ],
        flops=2 * own_rows * LANES * channels,
    )
    parts = [sent[0]] + [swap(sent[hop], hop) for hop in hops]

    slab = shaped((rows, LANES), bf16)
    features, turned, cot_slab = kernel_call(
        lambda *refs: slab_body(shards, width, cells, *refs),
        [slab, shaped((LANES + LENGTH_ROWS, rows), bf16), slab],
        [info, *parts],
        [
            pltpu.VMEM((shards, 2, own_rows, LANES), f32),
            pltpu.VMEM((rows, LANES), f32),
            pltpu.VMEM((rows, LANES), f32),
        ],
    )
    forward = kernel_call(
        lambda *refs: forward_body(shards, width, frames, height, *refs),
        [shaped((rows, LANES), f32)] + [slab] * (shards - 1),
        [info, features, flat_weight],
        [
            pltpu.VMEM((3, frames + 2, height + 2, columns, LANES), bf16),
            pltpu.VMEM((rows, 27 * LANES), bf16),
            pltpu.VMEM((shards, rows, LANES), f32),
            pltpu.VMEM((27 * LANES, channels), bf16),
            pltpu.SemaphoreType.DMA((3,)),
        ],
        flops=2 * rows * 27 * LANES * channels,
        anywhere=(2,),
    )
    own_sum, sum_sends = forward[0], forward[1:]
    sum_parts = [swap(sum_sends[hop - 1], hop) for hop in hops]
    turned, _ = fence(turned, sum_parts[0])
    line_one, line_three = along_line(turned, 1), along_line(turned, 3)
    turned_side = send(turned, to_side)
    own_sum, *sum_parts, turned, line_one, line_three, turned_side = fence(
        own_sum, *sum_parts, turned, line_one, line_three, turned_side
    )

    d_conv, terms, act = kernel_call(
        lambda *refs: norm_body(shards, width, frames, height, per_group, *refs),
        [slab, shaped((8, LANES), f32), slab],
        [
            info,
            own_sum,
            *sum_parts,
            gain.reshape(1, channels),
            bias.reshape(1, channels),
            cot_slab,
        ],
        [pltpu.VMEM((rows, LANES), f32)] * 2
        + [pltpu.VMEM((2, 1, channels), f32), pltpu.SemaphoreType.DMA((2,))],
        flops=rows * LANES * 40,
        anywhere=(5, 6),
    )
    same_one, same_three = along_line(d_conv, 1), along_line(d_conv, 3)
    side = send(d_conv, to_side_or_chip)
    chip = send(d_conv, to_chip_or_side)
    same_partner = send(d_conv, to_core)
    turned_odd = pack([line_one, line_three])
    turned_sides = send(turned_odd, to_side)
    d_conv, same_one, same_three, side, chip, same_partner, turned, turned_sides = fence(
        d_conv, same_one, same_three, side, chip, same_partner, turned, turned_sides
    )

    same_even = along_line(d_conv, 2)
    same_odd = pack([same_one, same_three])
    side_odd = send(same_odd, to_side_or_chip)
    chip_odd = send(same_odd, to_chip_or_side)
    cross = send(side, to_chip_or_side)
    side_partner = send(side, to_core)
    chip_partner = send(chip, to_core)
    same_odd_partner = send(same_odd, to_core)
    mixed = [side, chip, side_partner, chip_partner]
    joint = shaped((own_rows, 2 * LANES), bf16)
    small, *joint_sends = kernel_call(
        lambda *refs: input_grad_body(shards, width, frames, height, *refs),
        [shaped((BIT_ROWS, LANES), f32)] + [joint] * shards,
        [info, d_conv, same_partner, *mixed, flat_weight, act, terms, *parts],
        [
            pltpu.VMEM((rows, channels), bf16),
            pltpu.VMEM((3, frames, height, columns, LANES), f32),
            pltpu.VMEM((rows, LANES), f32),
            pltpu.VMEM((shards, own_rows, LANES), f32),
            pltpu.VMEM((rows, LANES), f32),
        ],
        flops=2 * rows * 27 * LANES * channels,
    )
    same_even, side_odd, chip_odd, cross, same_odd_partner, small, turned, *joint_sends = fence(
        same_even, side_odd, chip_odd, cross, same_odd_partner, small, turned, *joint_sends
    )

    side_even = send(same_even, to_side_or_chip)
    chip_even = send(same_even, to_chip_or_side)
    cross_odd = send(side_odd, to_chip_or_side)
    turned_even = along_line(turned, 2)
    joint_parts = [joint_sends[0]] + [swap(joint_sends[hop], hop) for hop in hops]
    same_even_partner = send(same_even, to_core)
    side_odd_partner = send(side_odd, to_core)
    chip_odd_partner = send(chip_odd, to_core)
    cross_partner = send(cross, to_core)
    small = small + send(small, to_side)
    side_even, chip_even, cross_odd, turned_even, small, *joint_parts = fence(
        side_even, chip_even, cross_odd, turned_even, small, *joint_parts
    )

    cross_even = send(side_even, to_chip_or_side)
    turned_side_even = send(turned_even, to_side)
    side_even_partner = send(side_even, to_core)
    chip_even_partner = send(chip_even, to_core)
    cross_odd_partner = send(cross_odd, to_core)
    small = small + send(small, lambda l, s, c, k: (l ^ 1, s, c, k))
    grad_hidden, decoded = kernel_call(
        lambda *refs: finish_body(shards, width, *refs),
        [shaped((own_rows, channels), bf16), slab],
        [info, *joint_parts],
        [pltpu.VMEM((shards, own_rows, LANES), f32), pltpu.VMEM((rows, LANES), f32)],
    )
    cross_even, turned_side_even, small, _, _ = fence(
        cross_even, turned_side_even, small, grad_hidden, decoded
    )

    cross_even_partner = send(cross_even, to_core)
    small = small + send(small, lambda l, s, c, k: (l ^ 2, s, c, k))
    small, cross_even_partner = fence(small, cross_even_partner)
    pieces = [d_conv, same_odd, same_even, side, side_odd, side_even]
    pieces += [chip, chip_odd, chip_even, cross, cross_odd, cross_even]
    pieces += [same_partner, same_odd_partner, same_even_partner]
    pieces += [side_partner, side_odd_partner, side_even_partner]
    pieces += [chip_partner, chip_odd_partner, chip_even_partner]
    pieces += [cross_partner, cross_odd_partner, cross_even_partner]
    groups = [turned, turned_odd, turned_even, turned_side, turned_sides, turned_side_even]
    grad_weight = weight_grad(info, groups, pieces, frames, height, channels)

    small_parts = [small] + [swap(small, hop) for hop in hops]
    grad_embed, grad_gain, grad_bias = kernel_call(
        lambda *refs: terms_body(shards, *refs),
        [shaped((CODE_BITS, channels), f32)] + [shaped((1, channels), f32)] * 2,
        [info, *small_parts],
    )
    return (
        decoded.reshape(1, frames, 2 * height, 2 * width, LANES),
        grad_hidden.reshape(1, frames, height, width, channels),
        grad_weight.transpose(1, 0, 2),
        grad_embed,
        grad_gain.reshape(channels),
        grad_bias.reshape(channels),
    )


def along_line(block, hop):
    return send(block, lambda l, s, c, k: (l + hop, s, c, k))


def weight_grad(info, groups, pieces, frames, height, channels):
    rows = pieces[0].shape[0]
    clips = 2 * len(groups[:3]) + 2
    vmem = pl.BlockSpec(memory_space=pltpu.VMEM)
    smem = pl.BlockSpec(memory_space=pltpu.SMEM)
    hbm = pl.BlockSpec(memory_space=pltpu.HBM)
    counts = [3 * clips * LANES, 2 * clips * LANES, 3 * clips // 2 * LANES]
    return pl.pallas_call(
        lambda *refs: weight_grad_body(frames, height, LANES // height, clips, *refs),
        out_shape=shaped((27, LANES, channels), f32),
        in_specs=[smem] + [vmem] * len(groups) + [hbm] * len(pieces),
        out_specs=hbm,
        scratch_shapes=[pltpu.VMEM((count, channels), bf16) for count in counts]
        + [
            pltpu.VMEM((3, 9, LANES, channels), f32),
            pltpu.VMEM((9 * LANES, counts[0]), bf16),
            pltpu.SMEM((clips * (frames + 1),), jnp.int32),
            pltpu.VMEM((counts[0], LANES), bf16),
            pltpu.VMEM((LANES, 9 * LANES), bf16),
            pltpu.VMEM((8, rows, LANES), bf16),
            pltpu.VMEM((8, 3, rows, LANES), bf16),
            pltpu.SemaphoreType.DMA((len(pieces),)),
            pltpu.SemaphoreType.DMA((3,)),
        ],
        compiler_params=pltpu.CompilerParams(vmem_limit_bytes=WIDE_LIMIT),
        cost_estimate=SMALL_COST,
    )(info, *groups, *pieces)


def extended(block, sides, width):
    for axis, dim in sides:
        count = lax.axis_size(axis)
        forward = [(i, i + 1) for i in range(count - 1)]
        backward = [(target, source) for source, target in forward]
        low = lax.ppermute(
            lax.slice_in_dim(block, block.shape[dim] - width, None, axis=dim), axis, forward
        )
        high = lax.ppermute(lax.slice_in_dim(block, 0, width, axis=dim), axis, backward)
        block = jnp.concatenate([low, block, high], axis=dim)
    return block


def forward_taps(padded, frames, height, width):
    taps = []
    for depth_tap in range(3):
        for row_tap in range(3):
            for col_tap in range(3):
                taps.append(
                    padded[
                        depth_tap : depth_tap + frames,
                        row_tap : row_tap + height,
                        col_tap : col_tap + width,
                    ]
                )
    return taps


def backward_taps(padded, frames, height, width):
    taps = []
    for depth_tap in range(3):
        for row_tap in range(3):
            for col_tap in range(3):
                taps.append(
                    padded[
                        2 - depth_tap : 2 - depth_tap + frames,
                        2 - row_tap : 2 - row_tap + height,
                        2 - col_tap : 2 - col_tap + width,
                    ]
                )
    return taps


def own_columns(rimmed, frames, height, width):
    padded = jnp.pad(rimmed, ((2, 0), (1, 1), (0, 0), (0, 0)))
    return jnp.stack(forward_taps(padded, frames, height, width), axis=3)


def slab_columns(spread, frames, height, slab_width):
    padded = jnp.pad(spread, ((2, 0), (1, 1), (1, 1), (0, 0)))
    return jnp.concatenate(forward_taps(padded, frames, height, slab_width), axis=3)


def by_gathers(codes, lengths, hidden, embed, conv_weight, gain, bias, cotangent):
    frames = codes.shape[1]
    height = codes.shape[2]
    width = codes.shape[3]
    share = conv_weight.shape[0]
    channels = conv_weight.shape[2]
    quarter = channels // 4
    shards = lax.axis_size("shard")
    slab_width = width * shards
    positions = frames * height * width
    groups = GROUPS
    per_group = channels // groups
    frame_mask = (jnp.arange(frames) < lengths[0]).astype(jnp.float32)
    mask_cells = frame_mask[:, None, None, None]
    mask_groups = frame_mask[:, None, None, None, None]
    powers = 2 ** jnp.arange(CODE_BITS, dtype=jnp.int32)
    bits = (codes[0][..., None] // powers % 2 * 2 - 1).astype(jnp.bfloat16)
    embedded = jnp.dot(
        bits.reshape(positions, CODE_BITS), embed, preferred_element_type=jnp.float32
    ).reshape(frames, height, width, channels)
    features = ((embedded + hidden[0].astype(jnp.float32)) * mask_cells).astype(jnp.bfloat16)
    rimmed = extended(features, (("shard", 2),), 1)
    own_patches = own_columns(rimmed, frames, height, width)
    conv_out = jnp.einsum(
        "frwtn,ntc->frwc",
        own_patches,
        lax.all_gather(conv_weight, "shard", axis=0, tiled=True),
        preferred_element_type=jnp.float32,
    )
    grouped = conv_out.reshape(frames, height, width, groups, per_group)
    sum_one, sum_two = lax.psum(
        (
            jnp.sum(grouped * mask_groups, axis=(0, 1, 2, 4)),
            jnp.sum(grouped * grouped * mask_groups, axis=(0, 1, 2, 4)),
        ),
        "shard",
    )
    count = lengths[0].astype(jnp.float32) * (height * width * shards * per_group)
    mean = sum_one / count
    variance = sum_two / count - mean * mean
    inv_std = lax.rsqrt(variance + eps_norm)
    gain_group = gain.reshape(groups, per_group)
    bias_group = bias.reshape(groups, per_group)
    normed = (grouped - mean[:, None]) * inv_std[:, None]
    pre = normed * gain_group + bias_group
    sigma = jax.nn.sigmoid(pre)
    activated = pre * sigma * mask_groups
    decoded = (
        activated.reshape(frames, height, width, 2, 2, quarter)
        .transpose(0, 1, 3, 2, 4, 5)
        .reshape(frames, 2 * height, 2 * width, quarter)
        .astype(jnp.bfloat16)[None]
    )
    upstream = (
        cotangent[0]
        .astype(jnp.float32)
        .reshape(frames, height, 2, width, 2, quarter)
        .transpose(0, 1, 3, 2, 4, 5)
        .reshape(frames, height, width, groups, per_group)
        * mask_groups
    )
    d_pre = upstream * sigma * (1.0 + pre * (1.0 - sigma))
    gain_term = jnp.sum(d_pre * normed, axis=(0, 1, 2)).reshape(channels)
    bias_term = jnp.sum(d_pre, axis=(0, 1, 2)).reshape(channels)
    d_norm = d_pre * gain_group
    tot_one, tot_two = lax.psum(
        (jnp.sum(d_norm, axis=(0, 1, 2, 4)), jnp.sum(d_norm * normed, axis=(0, 1, 2, 4))), "shard"
    )
    d_conv = (
        (
            inv_std[:, None]
            * (d_norm - tot_one[:, None] / count - normed * tot_two[:, None] / count)
            * mask_groups
        )
        .reshape(frames, height, width, channels)
        .astype(jnp.bfloat16)
    )
    spread_back = lax.all_to_all(features, "shard", split_axis=3, concat_axis=2, tiled=True)
    slab_back = slab_columns(spread_back, frames, height, slab_width)
    whole_grad = lax.all_gather(d_conv, "shard", axis=2, tiled=True)
    back_share = jnp.transpose(conv_weight, (2, 1, 0)).reshape(channels, 27 * share)
    tap_images = jnp.dot(
        whole_grad.reshape(-1, channels), back_share, preferred_element_type=jnp.float32
    ).reshape(frames, height, slab_width, 27 * share)
    padded_images = jnp.pad(tap_images, ((0, 2), (1, 1), (1, 1), (0, 0)))
    input_sum = jnp.zeros((frames, height, slab_width, share), jnp.float32)
    for tap_index, shifted in enumerate(backward_taps(padded_images, frames, height, slab_width)):
        input_sum = input_sum + shifted[..., tap_index * share : (tap_index + 1) * share]
    d_features = lax.all_to_all(
        input_sum.astype(jnp.bfloat16), "shard", split_axis=2, concat_axis=3, tiled=True
    )
    clip_part = jnp.einsum(
        "pk,pc->kc",
        slab_back.reshape(-1, 27 * share),
        whole_grad.reshape(-1, channels),
        preferred_element_type=jnp.float32,
    )
    weight_sum = clip_part.reshape(27, share, channels).transpose(1, 0, 2)
    grad_conv = lax.psum(weight_sum.astype(jnp.bfloat16), "dp").astype(jnp.float32)
    grad_hidden = d_features * mask_cells.astype(jnp.bfloat16)
    embed_term = jnp.dot(
        bits.reshape(positions, CODE_BITS).T,
        grad_hidden.reshape(positions, channels),
        preferred_element_type=jnp.float32,
    )
    grad_embed, grad_gain, grad_bias = lax.psum((embed_term, gain_term, bias_term), ("dp", "shard"))
    return (decoded, grad_hidden[None], grad_conv, grad_embed, grad_gain, grad_bias)


def on_device(codes, lengths, hidden, embed, conv_weight, gain, bias, cotangent):
    share = conv_weight.shape[0]
    block = codes.shape[2] * codes.shape[3] * lax.axis_size("shard")
    fits = share == LANES and block == LANES and lax.axis_size("shard") == 4
    plan = by_slices if fits and lax.axis_size("dp") == 8 else by_gathers
    return plan(codes, lengths, hidden, embed, conv_weight, gain, bias, cotangent)


def solution(mesh):
    return jax.shard_map(
        on_device,
        mesh=mesh,
        in_specs=(
            P("dp", None, None, "shard"),
            P("dp"),
            P("dp", None, None, "shard", None),
            P(),
            P("shard", None, None),
            P(),
            P(),
            P("dp", None, None, "shard", None),
        ),
        out_specs=(
            P("dp", None, None, "shard", None),
            P("dp", None, None, "shard", None),
            P("shard", None, None),
            P(),
            P(),
            P(),
        ),
        check_vma=False,
    )
```

```python
import math

import jax
import jax.numpy as jnp
from jax import lax
from jax.experimental import pallas as pl
from jax.experimental.pallas import tpu as pltpu
from jax.sharding import PartitionSpec as P

CODE_BITS = 18
GROUPS = 32
LANES = 128
LENGTH_ROWS = 16
BIT_ROWS = 32
TERM_ROW = 24
MIB = 1024 * 1024
WIDE_LIMIT = 61 * MIB
SMALL_COST = pl.CostEstimate(flops=1, bytes_accessed=1, transcendentals=0)

eps_norm = 1e-05

bf16 = jnp.bfloat16
f32 = jnp.float32


def scratch_bytes(scratch):
    held = [s for s in scratch if s.dtype in (bf16, f32)]
    return sum(math.prod(s.shape) * jnp.dtype(s.dtype).itemsize for s in held)


def kernel_call(body, outs, args, scratch=(), scalars=1, flops=0, anywhere=()):
    vmem = pl.BlockSpec(memory_space=pltpu.VMEM)
    specs = [pl.BlockSpec(memory_space=pltpu.SMEM)] * scalars
    specs += [vmem] * (len(args) - scalars)
    for place in anywhere:
        specs[place] = pl.BlockSpec(memory_space=pltpu.HBM)
    moved = sum(a.size * a.dtype.itemsize for a in args)
    moved += sum(o.size * o.dtype.itemsize for o in outs)
    limit = min(56 * MIB, moved + scratch_bytes(scratch) + 12 * MIB)
    if anywhere:
        limit = WIDE_LIMIT
    return pl.pallas_call(
        body,
        out_shape=outs,
        in_specs=specs,
        out_specs=[vmem] * len(outs),
        scratch_shapes=scratch,
        compiler_params=pltpu.CompilerParams(vmem_limit_bytes=limit),
        cost_estimate=SMALL_COST,
    )(*args)


def shaped(shape, dtype):
    return jax.ShapeDtypeStruct(shape, dtype)


def swap(block, hop):
    pairs = [(i, i ^ hop) for i in range(lax.axis_size("shard"))]
    return lax.ppermute(block, "shard", pairs)


def step_rows(slab, first, count, step):
    return slab[pl.ds(first, count, stride=step), :]

def frame_rows_below(rows, limit):
    return (lax.broadcasted_iota(jnp.int32, (rows, 1), 0) < limit).astype(f32)


def embed_body(shards, width, frame_rows, info, codes, hidden, embed, cot, *rest):
    sends, (chunks, cot_wide, part, table) = rest[:shards], rest[shards:]
    rows = codes.shape[0]
    cells = rows // width
    lanes = lax.broadcasted_iota(jnp.int32, (rows, LANES), 1)
    spread = jnp.broadcast_to(codes[...], (rows, LANES))
    bit = lax.bitwise_and(lax.shift_right_logical(spread, jnp.minimum(lanes, 31)), 1)
    bits = jnp.where(lanes < CODE_BITS, 2 * bit - 1, 0).astype(f32)
    turned_bits = jnp.concatenate(
        [bits.T[:BIT_ROWS], jnp.zeros((BIT_ROWS, 2 * LANES - rows), f32)], axis=1
    ).astype(bf16)
    bits = bits.astype(bf16)
    table[...] = jnp.zeros_like(table)
    table[:CODE_BITS, :] = embed[...]
    embedded = jnp.dot(bits, table[...], preferred_element_type=f32)
    mask = frame_rows_below(rows, info[0] * frame_rows)
    features = ((embedded + hidden[...].astype(f32)) * mask).astype(bf16)
    cot_wide[...] = cot[...].astype(f32)
    for j in range(shards):
        chunks[j, :rows, :LANES] = features[:, j * LANES : (j + 1) * LANES]
        for w in range(width):
            first = (j // 2) * (2 * width) + 2 * w + j % 2
            part[pl.ds(w, cells, stride=width), :] = step_rows(cot_wide, first, cells, 4 * width)
        chunks[j, :rows, LANES:] = part[...].astype(bf16)
        chunks[j, rows:, :] = turned_bits
    for hop in range(shards):
        sends[hop][...] = chunks[lax.bitwise_xor(info[1], hop)]


def stage_body(weight, gain, bias, weight_out, scale_out, sem):
    copy = pltpu.make_async_copy(weight, weight_out, sem.at[0])
    copy.start()
    scale_out[...] = jnp.zeros_like(scale_out)
    scale_out[0:1, :] = gain[...]
    scale_out[1:2, :] = bias[...]
    copy.wait()


def slab_body(shards, width, cells, info, *rest):
    parts, (slab_out, turned_out, cot_out) = rest[:shards], rest[shards : shards + 3]
    chunks, slab, cot = rest[shards + 3 :]
    columns = width * shards
    for hop in range(shards):
        origin = lax.bitwise_xor(info[1], hop)
        chunks[origin, 0] = parts[hop][: cells * width, :LANES].astype(f32)
        chunks[origin, 1] = parts[hop][: cells * width, LANES:].astype(f32)
    for j in range(shards):
        for w in range(width):
            place = pl.ds(width * j + w, cells, stride=columns)
            slab[place, :] = chunks[j, 0, pl.ds(w, cells, stride=width), :]
            cot[place, :] = chunks[j, 1, pl.ds(w, cells, stride=width), :]
    cot_out[...] = cot[...].astype(bf16)
    slab_out[...] = slab[...].astype(bf16)
    turned_out[:LANES, :] = slab[...].T.astype(bf16)
    rows = cells * columns
    turned_out[LANES:, :] = jnp.full((LENGTH_ROWS, rows), info[0].astype(f32)).astype(bf16)


def forward_body(shards, width, frames, height, far, info, slab, weight, *rest):
    outs, (rims, patches, sums) = rest[:2], rest[2:]
    columns = width * shards
    rows = frames * height * columns
    middle = slab[...].astype(f32)
    column = lax.broadcasted_iota(jnp.int32, (rows, 1), 0) % columns
    rims[...] = jnp.zeros_like(rims)
    shifted = (
        jnp.where(column > 0, pltpu.roll(middle, 1, 0), 0.0),
        middle,
        jnp.where(column < columns - 1, pltpu.roll(middle, rows - 1, 0), 0.0),
    )
    for dw in range(3):
        rims[dw, 2:, 1 : height + 1] = (
            shifted[dw].astype(bf16).reshape(frames, height, columns, LANES)
        )
    for dt in range(3):
        for dr in range(3):
            for dw in range(3):
                tap = (dt * 3 + dr) * 3 + dw
                patches[:, tap * LANES : (tap + 1) * LANES] = rims[
                    dw, dt : dt + frames, dr : dr + height
                ].reshape(rows, LANES)
    chip = lax.bitwise_xor(info[1] // 2, far)
    lanes = pl.ds(pl.multiple_of(chip * 2 * LANES, 2 * LANES), 2 * LANES)
    total = jnp.dot(patches[...], weight[:, lanes], preferred_element_type=f32)
    sums[0] = total[:, :LANES]
    sums[1] = total[:, LANES:]
    core = lax.bitwise_and(info[1], 1)
    outs[0][...] = sums[core].astype(outs[0].dtype)
    outs[1][...] = sums[1 - core].astype(bf16)


def group_total(values, per_group):
    lane = lax.broadcasted_iota(jnp.int32, values.shape, 1)
    step = 1
    while step < per_group:
        above = pltpu.roll(values, LANES - step, 1)
        below = pltpu.roll(values, step, 1)
        values = values + jnp.where(lax.bitwise_and(lane, step) == 0, above, below)
        step *= 2
    return values


def column_total(values):
    return jnp.broadcast_to(jnp.sum(values, axis=0, keepdims=True), (8, LANES))


def norm_body(shards, width, frames, height, per_group, info, *rest):
    own, parts = rest[0], rest[1:shards]
    scale, cot, d_conv_out, terms_out, act = rest[shards : shards + 5]
    conv, slope = rest[shards + 5 :]
    own_lanes = pl.ds(pl.multiple_of(info[1] * LANES, LANES), LANES)
    gain, bias = scale[0:1, own_lanes], scale[1:2, own_lanes]
    columns = width * shards
    block = height * columns
    length = info[0]
    sum_one = jnp.zeros((8, LANES), f32)
    sum_two = jnp.zeros((8, LANES), f32)
    for t in range(frames):
        span = pl.ds(t * block, block)
        values = own[span, :]
        for received in parts:
            values = values + received[span, :].astype(f32)
        conv[span, :] = values
        mask = (t < length).astype(f32)
        sum_one += column_total(values) * mask
        sum_two += column_total(values * values) * mask
    count = length.astype(f32) * (block * per_group)
    mean = group_total(sum_one, per_group) / count
    variance = group_total(sum_two, per_group) / count - mean * mean
    inv_std = lax.rsqrt(variance + eps_norm)[:1]
    mean = mean[:1]
    gain_sum = jnp.zeros((8, LANES), f32)
    bias_sum = jnp.zeros((8, LANES), f32)
    for t in range(frames):
        span = pl.ds(t * block, block)
        mask = (t < length).astype(f32)
        normed = (conv[span, :] - mean) * inv_std
        pre = normed * gain + bias
        sigma = jax.nn.sigmoid(pre)
        act[span, :] = (pre * sigma * mask).astype(bf16)
        d_pre = cot[span, :].astype(f32) * mask * sigma * (1.0 + pre * (1.0 - sigma))
        conv[span, :] = normed
        slope[span, :] = d_pre
        gain_sum += column_total(d_pre * normed)
        bias_sum += column_total(d_pre)
    row = lax.broadcasted_iota(jnp.int32, (8, LANES), 0)
    terms_out[...] = jnp.where(row == 0, gain_sum, jnp.where(row == 1, bias_sum, 0.0))
    tot_one = (group_total(bias_sum * gain, per_group) / count)[:1]
    tot_two = (group_total(gain_sum * gain, per_group) / count)[:1]
    for t in range(frames):
        span = pl.ds(t * block, block)
        mask = (t < length).astype(f32)
        d_norm = slope[span, :] * gain
        d_conv_out[span, :] = (
            inv_std * (d_norm - tot_one - conv[span, :] * tot_two) * mask
        ).astype(bf16)


def column_chunks(shards, width, cells, slab, part):
    for j in range(shards):
        for w in range(width):
            part[j, pl.ds(w, cells, stride=width), :] = step_rows(
                slab, width * j + w, cells, width * shards
            )


def input_grad_body(shards, width, frames, height, info, *rest):
    own, near, mixed = rest[0], rest[1], rest[2:6]
    weight, act, terms = rest[6:9]
    parts = rest[9 : 9 + shards]
    small_out = rest[9 + shards]
    sends = rest[10 + shards : 10 + 2 * shards]
    whole, sums, slab, part, wide = rest[10 + 2 * shards :]
    columns = width * shards
    rows = frames * height * columns
    cells = frames * height
    own_rows = cells * width
    core = lax.bitwise_and(info[1], 1)

    def place(piece, hop, when):
        @pl.when(when)
        def _():
            origin = lax.bitwise_xor(info[1], hop)
            lanes = pl.ds(pl.multiple_of(origin * LANES, LANES), LANES)
            whole[:, lanes] = piece[...]

    always = info[1] >= 0
    place(own, 0, always)
    place(near, 1, always)
    place(mixed[0], 2, core == 1)
    place(mixed[1], 2, core == 0)
    place(mixed[2], 3, core == 0)
    place(mixed[3], 3, core == 1)
    sums[...] = jnp.zeros_like(sums)
    for first in range(0, 27, 2):
        taps = min(2, 27 - first)
        images = lax.dot_general(
            whole[...],
            weight[first * LANES : (first + taps) * LANES, :],
            (((1,), (1,)), ((), ())),
            preferred_element_type=f32,
        )
        for tap in range(first, first + taps):
            dt, dr, dw = tap // 9, tap // 3 % 3, tap % 3
            image = images[:, (tap - first) * LANES : (tap - first + 1) * LANES]
            image = image.reshape(frames, height, columns, LANES)
            low, high = max(0, dr - 1), min(height, height + dr - 1)
            sums[dw, : frames - 2 + dt, low:high] += image[
                2 - dt :, low + 1 - dr : high + 1 - dr
            ]
    column = lax.broadcasted_iota(jnp.int32, (rows, 1), 0) % columns
    after = pltpu.roll(sums[0].reshape(rows, LANES), rows - 1, 0)
    before = pltpu.roll(sums[2].reshape(rows, LANES), 1, 0)
    total = sums[1].reshape(rows, LANES)
    total = total + jnp.where(column < columns - 1, after, 0.0)
    total = total + jnp.where(column > 0, before, 0.0)
    slab[...] = total * frame_rows_below(rows, info[0] * (height * columns))
    wide[...] = act[...].astype(f32)
    small = jnp.zeros((BIT_ROWS, LANES), f32)
    column_chunks(shards, width, cells, slab, part)
    for hop in range(shards):
        grad = part[lax.bitwise_xor(info[1], hop)].astype(bf16)
        sends[hop][:, :LANES] = grad
        bits = parts[hop][own_rows:, :own_rows]
        small += jnp.dot(bits, grad, preferred_element_type=f32)
    column_chunks(shards, width, cells, wide, part)
    for hop in range(shards):
        sends[hop][:, LANES:] = part[lax.bitwise_xor(info[1], hop)].astype(bf16)
    small_out[:TERM_ROW, :] = small[:TERM_ROW]
    small_out[TERM_ROW:, :] = terms[...]


def finish_body(shards, width, info, *rest):
    parts, (hidden_out, decoded_out, active, slab) = rest[:shards], rest[shards:]
    cells = parts[0].shape[0] // width
    for hop in range(shards):
        origin = lax.bitwise_xor(info[1], hop)
        lanes = pl.ds(pl.multiple_of(origin * LANES, LANES), LANES)
        hidden_out[:, lanes] = parts[hop][:, :LANES]
        active[origin] = parts[hop][:, LANES:].astype(f32)
    for j in range(shards):
        for w in range(width):
            first = (j // 2) * (2 * width) + 2 * w + j % 2
            slab[pl.ds(first, cells, stride=4 * width), :] = active[
                j, pl.ds(w, cells, stride=width), :
            ]
    decoded_out[...] = slab[...].astype(bf16)


def terms_body(shards, info, *rest):
    parts, (embed_out, gain_out, bias_out) = rest[:shards], rest[shards:]
    for hop in range(shards):
        origin = lax.bitwise_xor(info[1], hop)
        lanes = pl.ds(pl.multiple_of(origin * LANES, LANES), LANES)
        embed_out[:, lanes] = parts[hop][:CODE_BITS, :]
        gain_out[:, lanes] = parts[hop][TERM_ROW : TERM_ROW + 1, :]
        bias_out[:, lanes] = parts[hop][TERM_ROW + 1 : TERM_ROW + 2, :]


def slot_clip(info, slot, clips):
    lines = clips // 2
    line = lax.rem(info[2] // 2 + lines - slot % lines, lines)
    return 2 * line + lax.bitwise_xor(lax.rem(info[2], 2), slot // lines)


def by_hop(group):
    own, odd, even = group
    return [own, odd.at[0], even, odd.at[1]]


def fill_taps(frames, height, columns, info, groups, left, table, images, shifts):
    turned = by_hop(groups[:3]) + by_hop(groups[3:])
    clips = len(turned)
    block = height * columns
    source = lax.broadcasted_iota(jnp.int32, (block, block), 0)
    place = lax.broadcasted_iota(jnp.int32, (block, block), 1)
    row, column = place // columns, place % columns
    for dr in range(3):
        for dw in range(3):
            tap = dr * 3 + dw
            match = source == place + (dr - 1) * columns + dw - 1
            if dr == 0:
                match = jnp.logical_and(match, row > 0)
            if dr == 2:
                match = jnp.logical_and(match, row < height - 1)
            if dw == 0:
                match = jnp.logical_and(match, column > 0)
            if dw == 2:
                match = jnp.logical_and(match, column < columns - 1)
            shifts[:, tap * block : (tap + 1) * block] = match.astype(f32).astype(bf16)

    for slot in range(clips):
        length = jnp.max(turned[slot][LANES:, :LANES].astype(f32)).astype(jnp.int32)
        table[slot_clip(info, slot, clips)] = length
    early = jnp.int32(0)
    for clip in range(clips):
        early = early + jnp.maximum(table[clip] - 2, 0)
    first, middle = jnp.int32(0), early
    for clip in range(clips):
        length = table[clip]
        for t in range(frames):
            left_over = length - 1 - t
            at = jnp.where(left_over == 1, middle, first + t)
            table[clips + clip * frames + t] = jnp.where(left_over == 0, 2 * clips + clip, at)
        first = first + jnp.maximum(length - 2, 0)
        middle = middle + jnp.minimum(length - 1, 1)

    for slot in range(clips):
        clip = slot_clip(info, slot, clips)
        for t in range(frames):

            @pl.when(t < table[clip])
            def _(slot=slot, clip=clip, t=t):
                at = table[clips + clip * frames + t]
                there = pl.ds(pl.multiple_of(at * LANES, LANES), LANES)
                images[there, :] = turned[slot][:LANES, t * block : (t + 1) * block]

    step = 4
    for n in range(0, 3 * clips, step):
        moved = jnp.dot(
            images[n * LANES : (n + step) * LANES, :], shifts[...], preferred_element_type=f32
        ).astype(bf16)
        for frame in range(step):
            lanes = slice((n + frame) * block, (n + frame + 1) * block)
            for tap in range(9):
                left[tap * LANES : (tap + 1) * LANES, lanes] = moved[
                    frame * LANES : (frame + 1) * LANES, tap * block : (tap + 1) * block
                ]


def weight_grad_body(frames, height, columns, clips, info, *rest):
    groups, pieces, out = rest[:6], rest[6:30], rest[30]
    rights, (product, left, table, images, shifts, near, line) = rest[31:34], rest[34:41]
    in_sems, sems = rest[41:]
    block = height * columns
    fetches = []
    for kind in range(8):
        targets = near.at[kind], line.at[kind, pl.ds(0, 2)], line.at[kind, 2]
        for place, target in enumerate(targets):
            source = pieces[3 * kind + place]
            fetches.append(pltpu.make_async_copy(source, target, in_sems.at[3 * kind + place]))
            fetches[-1].start()
    fill_taps(frames, height, columns, info, groups, left, table, images, shifts)
    for fetch in fetches:
        fetch.wait()
    held = []
    for kind in range(8):
        held.append([near.at[kind], line.at[kind, 0], line.at[kind, 2], line.at[kind, 1]])
    lines = clips // 2
    core = lax.bitwise_and(info[1], 1)
    rights[2][clips * block :, :] = jnp.zeros_like(rights[2][clips * block :, :])

    def place(slot, t, mine):
        found = []
        for hop in range(2):
            same, side, chip, cross = (held[4 * hop + kind][slot % lines] for kind in range(4))
            if hop != mine:
                side, chip = chip, side
            found += [(hop, same), (hop + 2, chip)] if slot < lines else [
                (hop, side), (hop + 2, cross)
            ]
        clip = slot_clip(info, slot, clips)
        for hop, image in found:
            part = lax.bitwise_xor(info[1], hop)
            lanes = pl.ds(pl.multiple_of(part * LANES, LANES), LANES)
            value = image[t * block : (t + 1) * block, :]
            for lag in range(min(t + 1, 3)):
                at = table[clips + clip * frames + t - lag]
                there = pl.ds(pl.multiple_of(at * block, block), block)
                rights[lag][there, lanes] = value

    for mine in range(2):

        @pl.when(core == mine)
        def _(mine=mine):
            for slot in range(clips):
                for t in range(frames):

                    @pl.when(t < table[slot_clip(info, slot, clips)])
                    def _(slot=slot, t=t):
                        place(slot, t, mine)

    copies = []
    for lag in range(3):
        used = rights[lag].shape[0]
        product[2 - lag] = jnp.dot(
            left[:, :used], rights[lag][...], preferred_element_type=f32
        ).reshape(9, LANES, rights[lag].shape[1])
        copy = pltpu.make_async_copy(
            product.at[2 - lag], out.at[pl.ds((2 - lag) * 9, 9)], sems.at[lag]
        )
        copy.start()
        copies.append(copy)
    for copy in copies:
        copy.wait()


def pack(blocks):
    def body(*refs):
        for place, ref in enumerate(refs[:-1]):
            refs[-1][place] = ref[...]

    vmem = pl.BlockSpec(memory_space=pltpu.VMEM)
    size = len(blocks) * blocks[0].size
    return pl.pallas_call(
        body,
        out_shape=shaped((len(blocks), *blocks[0].shape), blocks[0].dtype),
        in_specs=[vmem] * len(blocks),
        out_specs=vmem,
        compiler_params=pltpu.CompilerParams(vmem_limit_bytes=4 * MIB),
        cost_estimate=SMALL_COST,
    )(*blocks)


def send(block, target):
    lines, shards = lax.axis_size("dp") // 2, lax.axis_size("shard")
    pairs = []
    for line in range(lines):
        for side in range(2):
            for chip in range(shards // 2):
                for core in range(2):
                    to_line, to_side, to_chip, to_core = target(line, side, chip, core)
                    source = (line * 2 + side) * shards + chip * 2 + core
                    sink = (to_line % lines * 2 + to_side) * shards + to_chip * 2 + to_core
                    pairs.append((source, sink))
    return lax.ppermute(block, ("dp", "shard"), pairs)


def to_side(line, side, chip, core):
    return line, 1 - side, chip, core


def to_chip(line, side, chip, core):
    return line, side, 1 - chip, core


def to_core(line, side, chip, core):
    return line, side, chip, 1 - core


def to_side_or_chip(line, side, chip, core):
    return (line, 1 - side, chip, core) if core == 0 else (line, side, 1 - chip, core)


def to_chip_or_side(line, side, chip, core):
    return (line, 1 - side, chip, core) if core == 1 else (line, side, 1 - chip, core)


def fence(*values):
    return lax.optimization_barrier(values)


def by_slices(codes, lengths, hidden, embed, conv_weight, gain, bias, cotangent):
    _, frames, height, width = codes.shape
    channels = conv_weight.shape[2]
    shards = lax.axis_size("shard")
    clips = lax.axis_size("dp")
    per_group = channels // GROUPS
    columns = width * shards
    cells = frames * height
    rows = cells * columns
    own_rows = cells * width
    block = height * columns
    here = lax.axis_index("shard")
    info = jnp.stack([lengths[0], here, lax.axis_index("dp")])
    hops = range(1, shards)
    flat_weight = conv_weight.transpose(1, 0, 2).reshape(27 * LANES, channels)

    chunk = shaped((own_rows + BIT_ROWS, 2 * LANES), bf16)
    sent = kernel_call(
        lambda *refs: embed_body(shards, width, height * width, *refs),
        [chunk] * shards,
        [
            info,
            codes.reshape(own_rows, 1),
            hidden.reshape(own_rows, channels),
            embed,
            cotangent.reshape(rows, LANES),
        ],
        [
            pltpu.VMEM((shards, own_rows + BIT_ROWS, 2 * LANES), bf16),
            pltpu.VMEM((rows, LANES), f32),
            pltpu.VMEM((own_rows, LANES), f32),
            pltpu.VMEM((LANES, channels), bf16),
        ],
        flops=2 * own_rows * LANES * channels,
    )
    parts = [sent[0]] + [swap(sent[hop], hop) for hop in hops]
    vmem = pl.BlockSpec(memory_space=pltpu.VMEM)
    held_weight, scale = pl.pallas_call(
        stage_body,
        out_shape=[shaped(flat_weight.shape, bf16), shaped((8, channels), f32)],
        in_specs=[pl.BlockSpec(memory_space=pltpu.HBM), vmem, vmem],
        out_specs=[vmem, vmem],
        scratch_shapes=[pltpu.SemaphoreType.DMA((1,))],
        compiler_params=pltpu.CompilerParams(vmem_limit_bytes=8 * MIB),
        cost_estimate=SMALL_COST,
    )(flat_weight, gain.reshape(1, channels), bias.reshape(1, channels))
    held_weight, scale, *parts = fence(held_weight, scale, *parts)

    slab = shaped((rows, LANES), bf16)
    features, turned, cot_slab = kernel_call(
        lambda *refs: slab_body(shards, width, cells, *refs),
        [slab, shaped((LANES + LENGTH_ROWS, rows), bf16), slab],
        [info, *parts],
        [
            pltpu.VMEM((shards, 2, own_rows, LANES), f32),
            pltpu.VMEM((rows, LANES), f32),
            pltpu.VMEM((rows, LANES), f32),
        ],
    )
    line_one, line_three = along_line(turned, 1), along_line(turned, 3)
    turned_side = send(turned, to_side)

    def forward_half(image, far, own_type):
        return kernel_call(
            lambda *refs: forward_body(shards, width, frames, height, far, *refs),
            [shaped((rows, LANES), own_type), slab],
            [info, image, held_weight],
            [
                pltpu.VMEM((3, frames + 2, height + 2, columns, LANES), bf16),
                pltpu.VMEM((rows, 27 * LANES), bf16),
                pltpu.VMEM((2, rows, LANES), f32),
            ],
            flops=rows * 27 * LANES * channels,
        )

    far_sends = forward_half(features, 1, bf16)
    features, turned, line_one, line_three, turned_side, _ = fence(
        features, turned, line_one, line_three, turned_side, far_sends[0]
    )
    own_sum, near_send = forward_half(features, 0, f32)
    sum_parts = [swap(near_send, 1), swap(far_sends[0], 2), swap(far_sends[1], 3)]

    d_conv, terms, act = kernel_call(
        lambda *refs: norm_body(shards, width, frames, height, per_group, *refs),
        [slab, shaped((8, LANES), f32), slab],
        [
            info,
            own_sum,
            *sum_parts,
            scale,
            cot_slab,
        ],
        [pltpu.VMEM((rows, LANES), f32)] * 2,
        flops=rows * LANES * 40,
    )
    same_one, same_three = along_line(d_conv, 1), along_line(d_conv, 3)
    side = send(d_conv, to_side_or_chip)
    chip = send(d_conv, to_chip_or_side)
    same_partner = send(d_conv, to_core)
    turned_odd = pack([line_one, line_three])
    turned_sides = send(turned_odd, to_side)
    d_conv, same_one, same_three, side, chip, same_partner, turned, turned_sides = fence(
        d_conv, same_one, same_three, side, chip, same_partner, turned, turned_sides
    )

    same_even = along_line(d_conv, 2)
    same_odd = pack([same_one, same_three])
    side_odd = send(same_odd, to_side_or_chip)
    chip_odd = send(same_odd, to_chip_or_side)
    cross = send(side, to_chip_or_side)
    side_partner = send(side, to_core)
    chip_partner = send(chip, to_core)
    same_odd_partner = send(same_odd, to_core)
    mixed = [side, chip, side_partner, chip_partner]
    joint = shaped((own_rows, 2 * LANES), bf16)
    small, *joint_sends = kernel_call(
        lambda *refs: input_grad_body(shards, width, frames, height, *refs),
        [shaped((BIT_ROWS, LANES), f32)] + [joint] * shards,
        [info, d_conv, same_partner, *mixed, held_weight, act, terms, *parts],
        [
            pltpu.VMEM((rows, channels), bf16),
            pltpu.VMEM((3, frames, height, columns, LANES), f32),
            pltpu.VMEM((rows, LANES), f32),
            pltpu.VMEM((shards, own_rows, LANES), f32),
            pltpu.VMEM((rows, LANES), f32),
        ],
        flops=2 * rows * 27 * LANES * channels,
    )
    same_even, side_odd, chip_odd, cross, same_odd_partner, small, turned, *joint_sends = fence(
        same_even, side_odd, chip_odd, cross, same_odd_partner, small, turned, *joint_sends
    )

    side_even = send(same_even, to_side_or_chip)
    chip_even = send(same_even, to_chip_or_side)
    cross_odd = send(side_odd, to_chip_or_side)
    turned_even = along_line(turned, 2)
    joint_parts = [joint_sends[0]] + [swap(joint_sends[hop], hop) for hop in hops]
    same_even_partner = send(same_even, to_core)
    side_odd_partner = send(side_odd, to_core)
    chip_odd_partner = send(chip_odd, to_core)
    cross_partner = send(cross, to_core)
    small = small + send(small, to_side)
    side_even, chip_even, cross_odd, turned_even, small, *joint_parts = fence(
        side_even, chip_even, cross_odd, turned_even, small, *joint_parts
    )

    cross_even = send(side_even, to_chip_or_side)
    turned_side_even = send(turned_even, to_side)
    side_even_partner = send(side_even, to_core)
    chip_even_partner = send(chip_even, to_core)
    cross_odd_partner = send(cross_odd, to_core)
    small = small + send(small, lambda l, s, c, k: (l ^ 1, s, c, k))
    grad_hidden, decoded = kernel_call(
        lambda *refs: finish_body(shards, width, *refs),
        [shaped((own_rows, channels), bf16), slab],
        [info, *joint_parts],
        [pltpu.VMEM((shards, own_rows, LANES), f32), pltpu.VMEM((rows, LANES), f32)],
    )
    cross_even, turned_side_even, small, _, _ = fence(
        cross_even, turned_side_even, small, grad_hidden, decoded
    )

    cross_even_partner = send(cross_even, to_core)
    pieces = [d_conv, same_odd, same_even, side, side_odd, side_even]
    pieces += [chip, chip_odd, chip_even, cross, cross_odd, cross_even]
    pieces += [same_partner, same_odd_partner, same_even_partner]
    pieces += [side_partner, side_odd_partner, side_even_partner]
    pieces += [chip_partner, chip_odd_partner, chip_even_partner]
    pieces += [cross_partner, cross_odd_partner, cross_even_partner]
    groups = [turned, turned_odd, turned_even, turned_side, turned_sides, turned_side_even]
    grad_weight = weight_grad(info, groups, pieces, frames, height, channels)

    small = small + send(small, lambda l, s, c, k: (l ^ 2, s, c, k))
    small_parts = [small] + [swap(small, hop) for hop in hops]
    grad_embed, grad_gain, grad_bias = kernel_call(
        lambda *refs: terms_body(shards, *refs),
        [shaped((CODE_BITS, channels), f32)] + [shaped((1, channels), f32)] * 2,
        [info, *small_parts],
    )
    return (
        decoded.reshape(1, frames, 2 * height, 2 * width, LANES),
        grad_hidden.reshape(1, frames, height, width, channels),
        grad_weight.transpose(1, 0, 2),
        grad_embed,
        grad_gain.reshape(channels),
        grad_bias.reshape(channels),
    )


def along_line(block, hop):
    return send(block, lambda l, s, c, k: (l + hop, s, c, k))


def weight_grad(info, groups, pieces, frames, height, channels):
    rows = pieces[0].shape[0]
    clips = 2 * len(groups[:3]) + 2
    vmem = pl.BlockSpec(memory_space=pltpu.VMEM)
    smem = pl.BlockSpec(memory_space=pltpu.SMEM)
    hbm = pl.BlockSpec(memory_space=pltpu.HBM)
    counts = [3 * clips * LANES, 2 * clips * LANES, 3 * clips // 2 * LANES]
    return pl.pallas_call(
        lambda *refs: weight_grad_body(frames, height, LANES // height, clips, *refs),
        out_shape=shaped((27, LANES, channels), f32),
        in_specs=[smem] + [vmem] * len(groups) + [hbm] * len(pieces),
        out_specs=hbm,
        scratch_shapes=[pltpu.VMEM((count, channels), bf16) for count in counts]
        + [
            pltpu.VMEM((3, 9, LANES, channels), f32),
            pltpu.VMEM((9 * LANES, counts[0]), bf16),
            pltpu.SMEM((clips * (frames + 1),), jnp.int32),
            pltpu.VMEM((counts[0], LANES), bf16),
            pltpu.VMEM((LANES, 9 * LANES), bf16),
            pltpu.VMEM((8, rows, LANES), bf16),
            pltpu.VMEM((8, 3, rows, LANES), bf16),
            pltpu.SemaphoreType.DMA((len(pieces),)),
            pltpu.SemaphoreType.DMA((3,)),
        ],
        compiler_params=pltpu.CompilerParams(vmem_limit_bytes=WIDE_LIMIT),
        cost_estimate=SMALL_COST,
    )(info, *groups, *pieces)


def extended(block, sides, width):
    for axis, dim in sides:
        count = lax.axis_size(axis)
        forward = [(i, i + 1) for i in range(count - 1)]
        backward = [(target, source) for source, target in forward]
        low = lax.ppermute(
            lax.slice_in_dim(block, block.shape[dim] - width, None, axis=dim), axis, forward
        )
        high = lax.ppermute(lax.slice_in_dim(block, 0, width, axis=dim), axis, backward)
        block = jnp.concatenate([low, block, high], axis=dim)
    return block


def forward_taps(padded, frames, height, width):
    taps = []
    for depth_tap in range(3):
        for row_tap in range(3):
            for col_tap in range(3):
                taps.append(
                    padded[
                        depth_tap : depth_tap + frames,
                        row_tap : row_tap + height,
                        col_tap : col_tap + width,
                    ]
                )
    return taps


def backward_taps(padded, frames, height, width):
    taps = []
    for depth_tap in range(3):
        for row_tap in range(3):
            for col_tap in range(3):
                taps.append(
                    padded[
                        2 - depth_tap : 2 - depth_tap + frames,
                        2 - row_tap : 2 - row_tap + height,
                        2 - col_tap : 2 - col_tap + width,
                    ]
                )
    return taps


def own_columns(rimmed, frames, height, width):
    padded = jnp.pad(rimmed, ((2, 0), (1, 1), (0, 0), (0, 0)))
    return jnp.stack(forward_taps(padded, frames, height, width), axis=3)


def slab_columns(spread, frames, height, slab_width):
    padded = jnp.pad(spread, ((2, 0), (1, 1), (1, 1), (0, 0)))
    return jnp.concatenate(forward_taps(padded, frames, height, slab_width), axis=3)


def by_gathers(codes, lengths, hidden, embed, conv_weight, gain, bias, cotangent):
    frames = codes.shape[1]
    height = codes.shape[2]
    width = codes.shape[3]
    share = conv_weight.shape[0]
    channels = conv_weight.shape[2]
    quarter = channels // 4
    shards = lax.axis_size("shard")
    slab_width = width * shards
    positions = frames * height * width
    groups = GROUPS
    per_group = channels // groups
    frame_mask = (jnp.arange(frames) < lengths[0]).astype(jnp.float32)
    mask_cells = frame_mask[:, None, None, None]
    mask_groups = frame_mask[:, None, None, None, None]
    powers = 2 ** jnp.arange(CODE_BITS, dtype=jnp.int32)
    bits = (codes[0][..., None] // powers % 2 * 2 - 1).astype(jnp.bfloat16)
    embedded = jnp.dot(
        bits.reshape(positions, CODE_BITS), embed, preferred_element_type=jnp.float32
    ).reshape(frames, height, width, channels)
    features = ((embedded + hidden[0].astype(jnp.float32)) * mask_cells).astype(jnp.bfloat16)
    rimmed = extended(features, (("shard", 2),), 1)
    own_patches = own_columns(rimmed, frames, height, width)
    conv_out = jnp.einsum(
        "frwtn,ntc->frwc",
        own_patches,
        lax.all_gather(conv_weight, "shard", axis=0, tiled=True),
        preferred_element_type=jnp.float32,
    )
    grouped = conv_out.reshape(frames, height, width, groups, per_group)
    sum_one, sum_two = lax.psum(
        (
            jnp.sum(grouped * mask_groups, axis=(0, 1, 2, 4)),
            jnp.sum(grouped * grouped * mask_groups, axis=(0, 1, 2, 4)),
        ),
        "shard",
    )
    count = lengths[0].astype(jnp.float32) * (height * width * shards * per_group)
    mean = sum_one / count
    variance = sum_two / count - mean * mean
    inv_std = lax.rsqrt(variance + eps_norm)
    gain_group = gain.reshape(groups, per_group)
    bias_group = bias.reshape(groups, per_group)
    normed = (grouped - mean[:, None]) * inv_std[:, None]
    pre = normed * gain_group + bias_group
    sigma = jax.nn.sigmoid(pre)
    activated = pre * sigma * mask_groups
    decoded = (
        activated.reshape(frames, height, width, 2, 2, quarter)
        .transpose(0, 1, 3, 2, 4, 5)
        .reshape(frames, 2 * height, 2 * width, quarter)
        .astype(jnp.bfloat16)[None]
    )
    upstream = (
        cotangent[0]
        .astype(jnp.float32)
        .reshape(frames, height, 2, width, 2, quarter)
        .transpose(0, 1, 3, 2, 4, 5)
        .reshape(frames, height, width, groups, per_group)
        * mask_groups
    )
    d_pre = upstream * sigma * (1.0 + pre * (1.0 - sigma))
    gain_term = jnp.sum(d_pre * normed, axis=(0, 1, 2)).reshape(channels)
    bias_term = jnp.sum(d_pre, axis=(0, 1, 2)).reshape(channels)
    d_norm = d_pre * gain_group
    tot_one, tot_two = lax.psum(
        (jnp.sum(d_norm, axis=(0, 1, 2, 4)), jnp.sum(d_norm * normed, axis=(0, 1, 2, 4))), "shard"
    )
    d_conv = (
        (
            inv_std[:, None]
            * (d_norm - tot_one[:, None] / count - normed * tot_two[:, None] / count)
            * mask_groups
        )
        .reshape(frames, height, width, channels)
        .astype(jnp.bfloat16)
    )
    spread_back = lax.all_to_all(features, "shard", split_axis=3, concat_axis=2, tiled=True)
    slab_back = slab_columns(spread_back, frames, height, slab_width)
    whole_grad = lax.all_gather(d_conv, "shard", axis=2, tiled=True)
    back_share = jnp.transpose(conv_weight, (2, 1, 0)).reshape(channels, 27 * share)
    tap_images = jnp.dot(
        whole_grad.reshape(-1, channels), back_share, preferred_element_type=jnp.float32
    ).reshape(frames, height, slab_width, 27 * share)
    padded_images = jnp.pad(tap_images, ((0, 2), (1, 1), (1, 1), (0, 0)))
    input_sum = jnp.zeros((frames, height, slab_width, share), jnp.float32)
    for tap_index, shifted in enumerate(backward_taps(padded_images, frames, height, slab_width)):
        input_sum = input_sum + shifted[..., tap_index * share : (tap_index + 1) * share]
    d_features = lax.all_to_all(
        input_sum.astype(jnp.bfloat16), "shard", split_axis=2, concat_axis=3, tiled=True
    )
    clip_part = jnp.einsum(
        "pk,pc->kc",
        slab_back.reshape(-1, 27 * share),
        whole_grad.reshape(-1, channels),
        preferred_element_type=jnp.float32,
    )
    weight_sum = clip_part.reshape(27, share, channels).transpose(1, 0, 2)
    grad_conv = lax.psum(weight_sum.astype(jnp.bfloat16), "dp").astype(jnp.float32)
    grad_hidden = d_features * mask_cells.astype(jnp.bfloat16)
    embed_term = jnp.dot(
        bits.reshape(positions, CODE_BITS).T,
        grad_hidden.reshape(positions, channels),
        preferred_element_type=jnp.float32,
    )
    grad_embed, grad_gain, grad_bias = lax.psum((embed_term, gain_term, bias_term), ("dp", "shard"))
    return (decoded, grad_hidden[None], grad_conv, grad_embed, grad_gain, grad_bias)


def on_device(codes, lengths, hidden, embed, conv_weight, gain, bias, cotangent):
    share = conv_weight.shape[0]
    block = codes.shape[2] * codes.shape[3] * lax.axis_size("shard")
    fits = share == LANES and block == LANES and lax.axis_size("shard") == 4
    plan = by_slices if fits and lax.axis_size("dp") == 8 else by_gathers
    return plan(codes, lengths, hidden, embed, conv_weight, gain, bias, cotangent)


def solution(mesh):
    return jax.shard_map(
        on_device,
        mesh=mesh,
        in_specs=(
            P("dp", None, None, "shard"),
            P("dp"),
            P("dp", None, None, "shard", None),
            P(),
            P("shard", None, None),
            P(),
            P(),
            P("dp", None, None, "shard", None),
        ),
        out_specs=(
            P("dp", None, None, "shard", None),
            P("dp", None, None, "shard", None),
            P("shard", None, None),
            P(),
            P(),
            P(),
        ),
        check_vma=False,
    )
```

```python
import math

import jax
import jax.numpy as jnp
from jax import lax
from jax.experimental import pallas as pl
from jax.experimental.pallas import tpu as pltpu
from jax.sharding import PartitionSpec as P

CODE_BITS = 18
GROUPS = 32
LANES = 128
LENGTH_ROWS = 16
BIT_ROWS = 32
TERM_ROW = 24
MIB = 1024 * 1024
WIDE_LIMIT = 61 * MIB
SMALL_COST = pl.CostEstimate(flops=1, bytes_accessed=1, transcendentals=0)

eps_norm = 1e-05

bf16 = jnp.bfloat16
f32 = jnp.float32


def scratch_bytes(scratch):
    held = [s for s in scratch if s.dtype in (bf16, f32)]
    return sum(math.prod(s.shape) * jnp.dtype(s.dtype).itemsize for s in held)


def kernel_call(body, outs, args, scratch=(), scalars=1, flops=0, anywhere=()):
    vmem = pl.BlockSpec(memory_space=pltpu.VMEM)
    specs = [pl.BlockSpec(memory_space=pltpu.SMEM)] * scalars
    specs += [vmem] * (len(args) - scalars)
    for place in anywhere:
        specs[place] = pl.BlockSpec(memory_space=pltpu.HBM)
    moved = sum(a.size * a.dtype.itemsize for a in args)
    moved += sum(o.size * o.dtype.itemsize for o in outs)
    limit = min(56 * MIB, moved + scratch_bytes(scratch) + 12 * MIB)
    if anywhere:
        limit = WIDE_LIMIT
    return pl.pallas_call(
        body,
        out_shape=outs,
        in_specs=specs,
        out_specs=[vmem] * len(outs),
        scratch_shapes=scratch,
        compiler_params=pltpu.CompilerParams(vmem_limit_bytes=limit),
        cost_estimate=SMALL_COST,
    )(*args)


def shaped(shape, dtype):
    return jax.ShapeDtypeStruct(shape, dtype)


def swap(block, hop):
    pairs = [(i, i ^ hop) for i in range(lax.axis_size("shard"))]
    return lax.ppermute(block, "shard", pairs)


def step_rows(slab, first, count, step):
    return slab[pl.ds(first, count, stride=step), :]

def frame_rows_below(rows, limit):
    return (lax.broadcasted_iota(jnp.int32, (rows, 1), 0) < limit).astype(f32)


def embed_body(shards, width, frame_rows, info, codes, hidden, embed, cot, *rest):
    sends, (chunks, cot_wide, part, table) = rest[:shards], rest[shards:]
    rows = codes.shape[0]
    cells = rows // width
    lanes = lax.broadcasted_iota(jnp.int32, (rows, LANES), 1)
    spread = jnp.broadcast_to(codes[...], (rows, LANES))
    bit = lax.bitwise_and(lax.shift_right_logical(spread, jnp.minimum(lanes, 31)), 1)
    bits = jnp.where(lanes < CODE_BITS, 2 * bit - 1, 0).astype(f32)
    turned_bits = jnp.concatenate(
        [bits.T[:BIT_ROWS], jnp.zeros((BIT_ROWS, 2 * LANES - rows), f32)], axis=1
    ).astype(bf16)
    bits = bits.astype(bf16)
    table[...] = jnp.zeros_like(table)
    table[:CODE_BITS, :] = embed[...]
    embedded = jnp.dot(bits, table[...], preferred_element_type=f32)
    mask = frame_rows_below(rows, info[0] * frame_rows)
    features = ((embedded + hidden[...].astype(f32)) * mask).astype(bf16)
    cot_wide[...] = cot[...].astype(f32)
    for j in range(shards):
        chunks[j, :rows, :LANES] = features[:, j * LANES : (j + 1) * LANES]
        for w in range(width):
            first = (j // 2) * (2 * width) + 2 * w + j % 2
            part[pl.ds(w, cells, stride=width), :] = step_rows(cot_wide, first, cells, 4 * width)
        chunks[j, :rows, LANES:] = part[...].astype(bf16)
        chunks[j, rows:, :] = turned_bits
    for hop in range(shards):
        sends[hop][...] = chunks[lax.bitwise_xor(info[1], hop)]


def stage_body(weight, gain, bias, weight_out, scale_out, sem):
    copy = pltpu.make_async_copy(weight, weight_out, sem.at[0])
    copy.start()
    scale_out[...] = jnp.zeros_like(scale_out)
    scale_out[0:1, :] = gain[...]
    scale_out[1:2, :] = bias[...]
    copy.wait()


def slab_body(shards, width, cells, info, *rest):
    parts, (slab_out, turned_out, cot_out) = rest[:shards], rest[shards : shards + 3]
    chunks, slab, cot = rest[shards + 3 :]
    columns = width * shards
    for hop in range(shards):
        origin = lax.bitwise_xor(info[1], hop)
        chunks[origin, 0] = parts[hop][: cells * width, :LANES].astype(f32)
        chunks[origin, 1] = parts[hop][: cells * width, LANES:].astype(f32)
    for j in range(shards):
        for w in range(width):
            place = pl.ds(width * j + w, cells, stride=columns)
            slab[place, :] = chunks[j, 0, pl.ds(w, cells, stride=width), :]
            cot[place, :] = chunks[j, 1, pl.ds(w, cells, stride=width), :]
    cot_out[...] = cot[...].astype(bf16)
    slab_out[...] = slab[...].astype(bf16)
    turned_out[:LANES, :] = slab[...].T.astype(bf16)
    rows = cells * columns
    turned_out[LANES:, :] = jnp.full((LENGTH_ROWS, rows), info[0].astype(f32)).astype(bf16)


def forward_body(shards, width, frames, height, far, info, slab, weight, *rest):
    outs, (rims, patches, sums) = rest[:2], rest[2:]
    columns = width * shards
    rows = frames * height * columns
    middle = slab[...].astype(f32)
    column = lax.broadcasted_iota(jnp.int32, (rows, 1), 0) % columns
    rims[...] = jnp.zeros_like(rims)
    shifted = (
        jnp.where(column > 0, pltpu.roll(middle, 1, 0), 0.0),
        middle,
        jnp.where(column < columns - 1, pltpu.roll(middle, rows - 1, 0), 0.0),
    )
    for dw in range(3):
        rims[dw, 2:, 1 : height + 1] = (
            shifted[dw].astype(bf16).reshape(frames, height, columns, LANES)
        )
    for dt in range(3):
        for dr in range(3):
            for dw in range(3):
                tap = (dt * 3 + dr) * 3 + dw
                patches[:, tap * LANES : (tap + 1) * LANES] = rims[
                    dw, dt : dt + frames, dr : dr + height
                ].reshape(rows, LANES)
    chip = lax.bitwise_xor(info[1] // 2, far)
    lanes = pl.ds(pl.multiple_of(chip * 2 * LANES, 2 * LANES), 2 * LANES)
    total = jnp.dot(patches[...], weight[:, lanes], preferred_element_type=f32)
    sums[0] = total[:, :LANES]
    sums[1] = total[:, LANES:]
    core = lax.bitwise_and(info[1], 1)
    outs[0][...] = sums[core].astype(outs[0].dtype)
    outs[1][...] = sums[1 - core].astype(bf16)


def group_total(values, per_group):
    lane = lax.broadcasted_iota(jnp.int32, values.shape, 1)
    step = 1
    while step < per_group:
        above = pltpu.roll(values, LANES - step, 1)
        below = pltpu.roll(values, step, 1)
        values = values + jnp.where(lax.bitwise_and(lane, step) == 0, above, below)
        step *= 2
    return values


def column_total(values):
    return jnp.broadcast_to(jnp.sum(values, axis=0, keepdims=True), (8, LANES))


def norm_body(shards, width, frames, height, per_group, info, *rest):
    own, parts = rest[0], rest[1:shards]
    scale, cot, d_conv_out, terms_out, act = rest[shards : shards + 5]
    conv, slope = rest[shards + 5 :]
    own_lanes = pl.ds(pl.multiple_of(info[1] * LANES, LANES), LANES)
    gain, bias = scale[0:1, own_lanes], scale[1:2, own_lanes]
    columns = width * shards
    block = height * columns
    length = info[0]
    sum_one = jnp.zeros((8, LANES), f32)
    sum_two = jnp.zeros((8, LANES), f32)
    for t in range(frames):
        span = pl.ds(t * block, block)
        values = own[span, :]
        for received in parts:
            values = values + received[span, :].astype(f32)
        conv[span, :] = values
        mask = (t < length).astype(f32)
        sum_one += column_total(values) * mask
        sum_two += column_total(values * values) * mask
    count = length.astype(f32) * (block * per_group)
    mean = group_total(sum_one, per_group) / count
    variance = group_total(sum_two, per_group) / count - mean * mean
    inv_std = lax.rsqrt(variance + eps_norm)[:1]
    mean = mean[:1]
    gain_sum = jnp.zeros((8, LANES), f32)
    bias_sum = jnp.zeros((8, LANES), f32)
    for t in range(frames):
        span = pl.ds(t * block, block)
        mask = (t < length).astype(f32)
        normed = (conv[span, :] - mean) * inv_std
        pre = normed * gain + bias
        sigma = jax.nn.sigmoid(pre)
        act[span, :] = (pre * sigma * mask).astype(bf16)
        d_pre = cot[span, :].astype(f32) * mask * sigma * (1.0 + pre * (1.0 - sigma))
        conv[span, :] = normed
        slope[span, :] = d_pre
        gain_sum += column_total(d_pre * normed)
        bias_sum += column_total(d_pre)
    row = lax.broadcasted_iota(jnp.int32, (8, LANES), 0)
    terms_out[...] = jnp.where(row == 0, gain_sum, jnp.where(row == 1, bias_sum, 0.0))
    tot_one = (group_total(bias_sum * gain, per_group) / count)[:1]
    tot_two = (group_total(gain_sum * gain, per_group) / count)[:1]
    for t in range(frames):
        span = pl.ds(t * block, block)
        mask = (t < length).astype(f32)
        d_norm = slope[span, :] * gain
        d_conv_out[span, :] = (
            inv_std * (d_norm - tot_one - conv[span, :] * tot_two) * mask
        ).astype(bf16)


def column_chunks(shards, width, cells, slab, part):
    for j in range(shards):
        for w in range(width):
            part[j, pl.ds(w, cells, stride=width), :] = step_rows(
                slab, width * j + w, cells, width * shards
            )


def input_grad_body(shards, width, frames, height, info, *rest):
    own, near, mixed = rest[0], rest[1], rest[2:6]
    weight, act, terms = rest[6:9]
    parts = rest[9 : 9 + shards]
    small_out = rest[9 + shards]
    sends = rest[10 + shards : 10 + 2 * shards]
    whole, sums, slab, part, wide = rest[10 + 2 * shards :]
    columns = width * shards
    rows = frames * height * columns
    cells = frames * height
    own_rows = cells * width
    core = lax.bitwise_and(info[1], 1)

    def place(piece, hop, when):
        @pl.when(when)
        def _():
            origin = lax.bitwise_xor(info[1], hop)
            lanes = pl.ds(pl.multiple_of(origin * LANES, LANES), LANES)
            whole[:, lanes] = piece[...]

    always = info[1] >= 0
    place(own, 0, always)
    place(near, 1, always)
    place(mixed[0], 2, core == 1)
    place(mixed[1], 2, core == 0)
    place(mixed[2], 3, core == 0)
    place(mixed[3], 3, core == 1)
    sums[...] = jnp.zeros_like(sums)
    for first in range(0, 27, 2):
        taps = min(2, 27 - first)
        images = lax.dot_general(
            whole[...],
            weight[first * LANES : (first + taps) * LANES, :],
            (((1,), (1,)), ((), ())),
            preferred_element_type=f32,
        )
        for tap in range(first, first + taps):
            dt, dr, dw = tap // 9, tap // 3 % 3, tap % 3
            image = images[:, (tap - first) * LANES : (tap - first + 1) * LANES]
            image = image.reshape(frames, height, columns, LANES)
            low, high = max(0, dr - 1), min(height, height + dr - 1)
            sums[dw, : frames - 2 + dt, low:high] += image[
                2 - dt :, low + 1 - dr : high + 1 - dr
            ]
    column = lax.broadcasted_iota(jnp.int32, (rows, 1), 0) % columns
    after = pltpu.roll(sums[0].reshape(rows, LANES), rows - 1, 0)
    before = pltpu.roll(sums[2].reshape(rows, LANES), 1, 0)
    total = sums[1].reshape(rows, LANES)
    total = total + jnp.where(column < columns - 1, after, 0.0)
    total = total + jnp.where(column > 0, before, 0.0)
    slab[...] = total * frame_rows_below(rows, info[0] * (height * columns))
    wide[...] = act[...].astype(f32)
    small = jnp.zeros((BIT_ROWS, LANES), f32)
    column_chunks(shards, width, cells, slab, part)
    for hop in range(shards):
        grad = part[lax.bitwise_xor(info[1], hop)].astype(bf16)
        sends[hop][:, :LANES] = grad
        bits = parts[hop][own_rows:, :own_rows]
        small += jnp.dot(bits, grad, preferred_element_type=f32)
    column_chunks(shards, width, cells, wide, part)
    for hop in range(shards):
        sends[hop][:, LANES:] = part[lax.bitwise_xor(info[1], hop)].astype(bf16)
    small_out[:TERM_ROW, :] = small[:TERM_ROW]
    small_out[TERM_ROW:, :] = terms[...]


def finish_body(shards, width, info, *rest):
    parts, (hidden_out, decoded_out, active, slab) = rest[:shards], rest[shards:]
    cells = parts[0].shape[0] // width
    for hop in range(shards):
        origin = lax.bitwise_xor(info[1], hop)
        lanes = pl.ds(pl.multiple_of(origin * LANES, LANES), LANES)
        hidden_out[:, lanes] = parts[hop][:, :LANES]
        active[origin] = parts[hop][:, LANES:].astype(f32)
    for j in range(shards):
        for w in range(width):
            first = (j // 2) * (2 * width) + 2 * w + j % 2
            slab[pl.ds(first, cells, stride=4 * width), :] = active[
                j, pl.ds(w, cells, stride=width), :
            ]
    decoded_out[...] = slab[...].astype(bf16)


def terms_body(shards, info, *rest):
    parts, (embed_out, gain_out, bias_out) = rest[:shards], rest[shards:]
    for hop in range(shards):
        origin = lax.bitwise_xor(info[1], hop)
        lanes = pl.ds(pl.multiple_of(origin * LANES, LANES), LANES)
        embed_out[:, lanes] = parts[hop][:CODE_BITS, :]
        gain_out[:, lanes] = parts[hop][TERM_ROW : TERM_ROW + 1, :]
        bias_out[:, lanes] = parts[hop][TERM_ROW + 1 : TERM_ROW + 2, :]


def slot_clip(info, slot, clips):
    lines = clips // 2
    line = lax.rem(info[2] // 2 + lines - slot % lines, lines)
    return 2 * line + lax.bitwise_xor(lax.rem(info[2], 2), slot // lines)


def by_hop(group):
    own, odd, even = group
    return [own, odd.at[0], even, odd.at[1]]


def fill_taps(frames, height, columns, info, groups, left, table, images, shifts):
    turned = by_hop(groups[:3]) + by_hop(groups[3:])
    clips = len(turned)
    block = height * columns
    source = lax.broadcasted_iota(jnp.int32, (block, block), 0)
    place = lax.broadcasted_iota(jnp.int32, (block, block), 1)
    row, column = place // columns, place % columns
    for dr in range(3):
        for dw in range(3):
            tap = dr * 3 + dw
            match = source == place + (dr - 1) * columns + dw - 1
            if dr == 0:
                match = jnp.logical_and(match, row > 0)
            if dr == 2:
                match = jnp.logical_and(match, row < height - 1)
            if dw == 0:
                match = jnp.logical_and(match, column > 0)
            if dw == 2:
                match = jnp.logical_and(match, column < columns - 1)
            shifts[:, tap * block : (tap + 1) * block] = match.astype(f32).astype(bf16)

    for slot in range(clips):
        length = jnp.max(turned[slot][LANES:, :LANES].astype(f32)).astype(jnp.int32)
        table[slot_clip(info, slot, clips)] = length
    early = jnp.int32(0)
    for clip in range(clips):
        early = early + jnp.maximum(table[clip] - 2, 0)
    first, middle = jnp.int32(0), early
    for clip in range(clips):
        length = table[clip]
        for t in range(frames):
            left_over = length - 1 - t
            at = jnp.where(left_over == 1, middle, first + t)
            table[clips + clip * frames + t] = jnp.where(left_over == 0, 2 * clips + clip, at)
        first = first + jnp.maximum(length - 2, 0)
        middle = middle + jnp.minimum(length - 1, 1)

    for slot in range(clips):
        clip = slot_clip(info, slot, clips)
        for t in range(frames):

            @pl.when(t < table[clip])
            def _(slot=slot, clip=clip, t=t):
                at = table[clips + clip * frames + t]
                there = pl.ds(pl.multiple_of(at * LANES, LANES), LANES)
                images[there, :] = turned[slot][:LANES, t * block : (t + 1) * block]

    step = 8
    for n in range(0, 3 * clips, step):
        moved = jnp.dot(
            images[n * LANES : (n + step) * LANES, :], shifts[...], preferred_element_type=f32
        ).astype(bf16)
        for frame in range(step):
            lanes = slice((n + frame) * block, (n + frame + 1) * block)
            for tap in range(9):
                left[tap * LANES : (tap + 1) * LANES, lanes] = moved[
                    frame * LANES : (frame + 1) * LANES, tap * block : (tap + 1) * block
                ]


def weight_grad_body(frames, height, columns, clips, info, *rest):
    groups, pieces, out = rest[:6], rest[6:30], rest[30]
    rights, (product, left, table, images, shifts, near, line) = rest[31:34], rest[34:41]
    in_sems, sems = rest[41:]
    block = height * columns
    fetches = []
    for kind in range(8):
        targets = near.at[kind], line.at[kind, pl.ds(0, 2)], line.at[kind, 2]
        for place, target in enumerate(targets):
            source = pieces[3 * kind + place]
            fetches.append(pltpu.make_async_copy(source, target, in_sems.at[3 * kind + place]))
            fetches[-1].start()
    fill_taps(frames, height, columns, info, groups, left, table, images, shifts)
    for fetch in fetches:
        fetch.wait()
    held = []
    for kind in range(8):
        held.append([near.at[kind], line.at[kind, 0], line.at[kind, 2], line.at[kind, 1]])
    lines = clips // 2
    core = lax.bitwise_and(info[1], 1)
    rights[2][clips * block :, :] = jnp.zeros_like(rights[2][clips * block :, :])

    def place(slot, t, mine):
        found = []
        for hop in range(2):
            same, side, chip, cross = (held[4 * hop + kind][slot % lines] for kind in range(4))
            if hop != mine:
                side, chip = chip, side
            found += [(hop, same), (hop + 2, chip)] if slot < lines else [
                (hop, side), (hop + 2, cross)
            ]
        clip = slot_clip(info, slot, clips)
        for hop, image in found:
            part = lax.bitwise_xor(info[1], hop)
            lanes = pl.ds(pl.multiple_of(part * LANES, LANES), LANES)
            value = image[t * block : (t + 1) * block, :]
            for lag in range(min(t + 1, 3)):
                at = table[clips + clip * frames + t - lag]
                there = pl.ds(pl.multiple_of(at * block, block), block)
                rights[lag][there, lanes] = value

    for mine in range(2):

        @pl.when(core == mine)
        def _(mine=mine):
            for slot in range(clips):
                place(slot, 0, mine)
                for t in range(1, frames):

                    @pl.when(t < table[slot_clip(info, slot, clips)])
                    def _(slot=slot, t=t):
                        place(slot, t, mine)

    copies = []
    for lag in range(3):
        used = rights[lag].shape[0]
        product[2 - lag] = jnp.dot(
            left[:, :used], rights[lag][...], preferred_element_type=f32
        ).reshape(9, LANES, rights[lag].shape[1])
        copy = pltpu.make_async_copy(
            product.at[2 - lag], out.at[pl.ds((2 - lag) * 9, 9)], sems.at[lag]
        )
        copy.start()
        copies.append(copy)
    for copy in copies:
        copy.wait()


def pack(blocks):
    def body(*refs):
        for place, ref in enumerate(refs[:-1]):
            refs[-1][place] = ref[...]

    vmem = pl.BlockSpec(memory_space=pltpu.VMEM)
    size = len(blocks) * blocks[0].size
    return pl.pallas_call(
        body,
        out_shape=shaped((len(blocks), *blocks[0].shape), blocks[0].dtype),
        in_specs=[vmem] * len(blocks),
        out_specs=vmem,
        compiler_params=pltpu.CompilerParams(vmem_limit_bytes=4 * MIB),
        cost_estimate=SMALL_COST,
    )(*blocks)


def send(block, target):
    lines, shards = lax.axis_size("dp") // 2, lax.axis_size("shard")
    pairs = []
    for line in range(lines):
        for side in range(2):
            for chip in range(shards // 2):
                for core in range(2):
                    to_line, to_side, to_chip, to_core = target(line, side, chip, core)
                    source = (line * 2 + side) * shards + chip * 2 + core
                    sink = (to_line % lines * 2 + to_side) * shards + to_chip * 2 + to_core
                    pairs.append((source, sink))
    return lax.ppermute(block, ("dp", "shard"), pairs)


def to_side(line, side, chip, core):
    return line, 1 - side, chip, core


def to_chip(line, side, chip, core):
    return line, side, 1 - chip, core


def to_core(line, side, chip, core):
    return line, side, chip, 1 - core


def to_side_or_chip(line, side, chip, core):
    return (line, 1 - side, chip, core) if core == 0 else (line, side, 1 - chip, core)


def to_chip_or_side(line, side, chip, core):
    return (line, 1 - side, chip, core) if core == 1 else (line, side, 1 - chip, core)


def fence(*values):
    return lax.optimization_barrier(values)


def by_slices(codes, lengths, hidden, embed, conv_weight, gain, bias, cotangent):
    _, frames, height, width = codes.shape
    channels = conv_weight.shape[2]
    shards = lax.axis_size("shard")
    clips = lax.axis_size("dp")
    per_group = channels // GROUPS
    columns = width * shards
    cells = frames * height
    rows = cells * columns
    own_rows = cells * width
    block = height * columns
    here = lax.axis_index("shard")
    info = jnp.stack([lengths[0], here, lax.axis_index("dp")])
    hops = range(1, shards)
    flat_weight = conv_weight.transpose(1, 0, 2).reshape(27 * LANES, channels)

    chunk = shaped((own_rows + BIT_ROWS, 2 * LANES), bf16)
    sent = kernel_call(
        lambda *refs: embed_body(shards, width, height * width, *refs),
        [chunk] * shards,
        [
            info,
            codes.reshape(own_rows, 1),
            hidden.reshape(own_rows, channels),
            embed,
            cotangent.reshape(rows, LANES),
        ],
        [
            pltpu.VMEM((shards, own_rows + BIT_ROWS, 2 * LANES), bf16),
            pltpu.VMEM((rows, LANES), f32),
            pltpu.VMEM((own_rows, LANES), f32),
            pltpu.VMEM((LANES, channels), bf16),
        ],
        flops=2 * own_rows * LANES * channels,
    )
    parts = [sent[0]] + [swap(sent[hop], hop) for hop in hops]
    vmem = pl.BlockSpec(memory_space=pltpu.VMEM)
    held_weight, scale = pl.pallas_call(
        stage_body,
        out_shape=[shaped(flat_weight.shape, bf16), shaped((8, channels), f32)],
        in_specs=[pl.BlockSpec(memory_space=pltpu.HBM), vmem, vmem],
        out_specs=[vmem, vmem],
        scratch_shapes=[pltpu.SemaphoreType.DMA((1,))],
        compiler_params=pltpu.CompilerParams(vmem_limit_bytes=8 * MIB),
        cost_estimate=SMALL_COST,
    )(flat_weight, gain.reshape(1, channels), bias.reshape(1, channels))
    held_weight, scale, *parts = fence(held_weight, scale, *parts)

    slab = shaped((rows, LANES), bf16)
    features, turned, cot_slab = kernel_call(
        lambda *refs: slab_body(shards, width, cells, *refs),
        [slab, shaped((LANES + LENGTH_ROWS, rows), bf16), slab],
        [info, *parts],
        [
            pltpu.VMEM((shards, 2, own_rows, LANES), f32),
            pltpu.VMEM((rows, LANES), f32),
            pltpu.VMEM((rows, LANES), f32),
        ],
    )
    line_one, line_three = along_line(turned, 1), along_line(turned, 3)
    turned_side = send(turned, to_side)

    def forward_half(image, far, own_type):
        return kernel_call(
            lambda *refs: forward_body(shards, width, frames, height, far, *refs),
            [shaped((rows, LANES), own_type), slab],
            [info, image, held_weight],
            [
                pltpu.VMEM((3, frames + 2, height + 2, columns, LANES), bf16),
                pltpu.VMEM((rows, 27 * LANES), bf16),
                pltpu.VMEM((2, rows, LANES), f32),
            ],
            flops=rows * 27 * LANES * channels,
        )

    far_sends = forward_half(features, 1, bf16)
    features, turned, line_one, line_three, turned_side, _ = fence(
        features, turned, line_one, line_three, turned_side, far_sends[0]
    )
    own_sum, near_send = forward_half(features, 0, f32)
    sum_parts = [swap(near_send, 1), swap(far_sends[0], 2), swap(far_sends[1], 3)]

    d_conv, terms, act = kernel_call(
        lambda *refs: norm_body(shards, width, frames, height, per_group, *refs),
        [slab, shaped((8, LANES), f32), slab],
        [
            info,
            own_sum,
            *sum_parts,
            scale,
            cot_slab,
        ],
        [pltpu.VMEM((rows, LANES), f32)] * 2,
        flops=rows * LANES * 40,
    )
    same_one, same_three = along_line(d_conv, 1), along_line(d_conv, 3)
    side = send(d_conv, to_side_or_chip)
    chip = send(d_conv, to_chip_or_side)
    same_partner = send(d_conv, to_core)
    turned_odd = pack([line_one, line_three])
    turned_sides = send(turned_odd, to_side)
    d_conv, same_one, same_three, side, chip, same_partner, turned, turned_sides = fence(
        d_conv, same_one, same_three, side, chip, same_partner, turned, turned_sides
    )

    same_even = along_line(d_conv, 2)
    same_odd = pack([same_one, same_three])
    side_odd = send(same_odd, to_side_or_chip)
    chip_odd = send(same_odd, to_chip_or_side)
    cross = send(side, to_chip_or_side)
    side_partner = send(side, to_core)
    chip_partner = send(chip, to_core)
    same_odd_partner = send(same_odd, to_core)
    mixed = [side, chip, side_partner, chip_partner]
    joint = shaped((own_rows, 2 * LANES), bf16)
    small, *joint_sends = kernel_call(
        lambda *refs: input_grad_body(shards, width, frames, height, *refs),
        [shaped((BIT_ROWS, LANES), f32)] + [joint] * shards,
        [info, d_conv, same_partner, *mixed, held_weight, act, terms, *parts],
        [
            pltpu.VMEM((rows, channels), bf16),
            pltpu.VMEM((3, frames, height, columns, LANES), f32),
            pltpu.VMEM((rows, LANES), f32),
            pltpu.VMEM((shards, own_rows, LANES), f32),
            pltpu.VMEM((rows, LANES), f32),
        ],
        flops=2 * rows * 27 * LANES * channels,
    )
    same_even, side_odd, chip_odd, cross, same_odd_partner, small, turned, *joint_sends = fence(
        same_even, side_odd, chip_odd, cross, same_odd_partner, small, turned, *joint_sends
    )

    side_even = send(same_even, to_side_or_chip)
    chip_even = send(same_even, to_chip_or_side)
    cross_odd = send(side_odd, to_chip_or_side)
    turned_even = along_line(turned, 2)
    joint_parts = [joint_sends[0]] + [swap(joint_sends[hop], hop) for hop in hops]
    same_even_partner = send(same_even, to_core)
    side_odd_partner = send(side_odd, to_core)
    chip_odd_partner = send(chip_odd, to_core)
    cross_partner = send(cross, to_core)
    small = small + send(small, to_side)
    side_even, chip_even, cross_odd, turned_even, small, *joint_parts = fence(
        side_even, chip_even, cross_odd, turned_even, small, *joint_parts
    )

    cross_even = send(side_even, to_chip_or_side)
    turned_side_even = send(turned_even, to_side)
    side_even_partner = send(side_even, to_core)
    chip_even_partner = send(chip_even, to_core)
    cross_odd_partner = send(cross_odd, to_core)
    small = small + send(small, lambda l, s, c, k: (l ^ 1, s, c, k))
    grad_hidden, decoded = kernel_call(
        lambda *refs: finish_body(shards, width, *refs),
        [shaped((own_rows, channels), bf16), slab],
        [info, *joint_parts],
        [pltpu.VMEM((shards, own_rows, LANES), f32), pltpu.VMEM((rows, LANES), f32)],
    )
    cross_even, turned_side_even, small, _, _ = fence(
        cross_even, turned_side_even, small, grad_hidden, decoded
    )

    cross_even_partner = send(cross_even, to_core)
    pieces = [d_conv, same_odd, same_even, side, side_odd, side_even]
    pieces += [chip, chip_odd, chip_even, cross, cross_odd, cross_even]
    pieces += [same_partner, same_odd_partner, same_even_partner]
    pieces += [side_partner, side_odd_partner, side_even_partner]
    pieces += [chip_partner, chip_odd_partner, chip_even_partner]
    pieces += [cross_partner, cross_odd_partner, cross_even_partner]
    groups = [turned, turned_odd, turned_even, turned_side, turned_sides, turned_side_even]
    grad_weight = weight_grad(info, groups, pieces, frames, height, channels)

    small = small + send(small, lambda l, s, c, k: (l ^ 2, s, c, k))
    small_parts = [small] + [swap(small, hop) for hop in hops]
    grad_embed, grad_gain, grad_bias = kernel_call(
        lambda *refs: terms_body(shards, *refs),
        [shaped((CODE_BITS, channels), f32)] + [shaped((1, channels), f32)] * 2,
        [info, *small_parts],
    )
    return (
        decoded.reshape(1, frames, 2 * height, 2 * width, LANES),
        grad_hidden.reshape(1, frames, height, width, channels),
        grad_weight.transpose(1, 0, 2),
        grad_embed,
        grad_gain.reshape(channels),
        grad_bias.reshape(channels),
    )


def along_line(block, hop):
    return send(block, lambda l, s, c, k: (l + hop, s, c, k))


def weight_grad(info, groups, pieces, frames, height, channels):
    rows = pieces[0].shape[0]
    clips = 2 * len(groups[:3]) + 2
    vmem = pl.BlockSpec(memory_space=pltpu.VMEM)
    smem = pl.BlockSpec(memory_space=pltpu.SMEM)
    hbm = pl.BlockSpec(memory_space=pltpu.HBM)
    counts = [3 * clips * LANES, 2 * clips * LANES, 3 * clips // 2 * LANES]
    return pl.pallas_call(
        lambda *refs: weight_grad_body(frames, height, LANES // height, clips, *refs),
        out_shape=shaped((27, LANES, channels), f32),
        in_specs=[smem] + [vmem] * len(groups) + [hbm] * len(pieces),
        out_specs=hbm,
        scratch_shapes=[pltpu.VMEM((count, channels), bf16) for count in counts]
        + [
            pltpu.VMEM((3, 9, LANES, channels), f32),
            pltpu.VMEM((9 * LANES, counts[0]), bf16),
            pltpu.SMEM((clips * (frames + 1),), jnp.int32),
            pltpu.VMEM((counts[0], LANES), bf16),
            pltpu.VMEM((LANES, 9 * LANES), bf16),
            pltpu.VMEM((8, rows, LANES), bf16),
            pltpu.VMEM((8, 3, rows, LANES), bf16),
            pltpu.SemaphoreType.DMA((len(pieces),)),
            pltpu.SemaphoreType.DMA((3,)),
        ],
        compiler_params=pltpu.CompilerParams(vmem_limit_bytes=WIDE_LIMIT),
        cost_estimate=SMALL_COST,
    )(info, *groups, *pieces)


def extended(block, sides, width):
    for axis, dim in sides:
        count = lax.axis_size(axis)
        forward = [(i, i + 1) for i in range(count - 1)]
        backward = [(target, source) for source, target in forward]
        low = lax.ppermute(
            lax.slice_in_dim(block, block.shape[dim] - width, None, axis=dim), axis, forward
        )
        high = lax.ppermute(lax.slice_in_dim(block, 0, width, axis=dim), axis, backward)
        block = jnp.concatenate([low, block, high], axis=dim)
    return block


def forward_taps(padded, frames, height, width):
    taps = []
    for depth_tap in range(3):
        for row_tap in range(3):
            for col_tap in range(3):
                taps.append(
                    padded[
                        depth_tap : depth_tap + frames,
                        row_tap : row_tap + height,
                        col_tap : col_tap + width,
                    ]
                )
    return taps


def backward_taps(padded, frames, height, width):
    taps = []
    for depth_tap in range(3):
        for row_tap in range(3):
            for col_tap in range(3):
                taps.append(
                    padded[
                        2 - depth_tap : 2 - depth_tap + frames,
                        2 - row_tap : 2 - row_tap + height,
                        2 - col_tap : 2 - col_tap + width,
                    ]
                )
    return taps


def own_columns(rimmed, frames, height, width):
    padded = jnp.pad(rimmed, ((2, 0), (1, 1), (0, 0), (0, 0)))
    return jnp.stack(forward_taps(padded, frames, height, width), axis=3)


def slab_columns(spread, frames, height, slab_width):
    padded = jnp.pad(spread, ((2, 0), (1, 1), (1, 1), (0, 0)))
    return jnp.concatenate(forward_taps(padded, frames, height, slab_width), axis=3)


def by_gathers(codes, lengths, hidden, embed, conv_weight, gain, bias, cotangent):
    frames = codes.shape[1]
    height = codes.shape[2]
    width = codes.shape[3]
    share = conv_weight.shape[0]
    channels = conv_weight.shape[2]
    quarter = channels // 4
    shards = lax.axis_size("shard")
    slab_width = width * shards
    positions = frames * height * width
    groups = GROUPS
    per_group = channels // groups
    frame_mask = (jnp.arange(frames) < lengths[0]).astype(jnp.float32)
    mask_cells = frame_mask[:, None, None, None]
    mask_groups = frame_mask[:, None, None, None, None]
    powers = 2 ** jnp.arange(CODE_BITS, dtype=jnp.int32)
    bits = (codes[0][..., None] // powers % 2 * 2 - 1).astype(jnp.bfloat16)
    embedded = jnp.dot(
        bits.reshape(positions, CODE_BITS), embed, preferred_element_type=jnp.float32
    ).reshape(frames, height, width, channels)
    features = ((embedded + hidden[0].astype(jnp.float32)) * mask_cells).astype(jnp.bfloat16)
    rimmed = extended(features, (("shard", 2),), 1)
    own_patches = own_columns(rimmed, frames, height, width)
    conv_out = jnp.einsum(
        "frwtn,ntc->frwc",
        own_patches,
        lax.all_gather(conv_weight, "shard", axis=0, tiled=True),
        preferred_element_type=jnp.float32,
    )
    grouped = conv_out.reshape(frames, height, width, groups, per_group)
    sum_one, sum_two = lax.psum(
        (
            jnp.sum(grouped * mask_groups, axis=(0, 1, 2, 4)),
            jnp.sum(grouped * grouped * mask_groups, axis=(0, 1, 2, 4)),
        ),
        "shard",
    )
    count = lengths[0].astype(jnp.float32) * (height * width * shards * per_group)
    mean = sum_one / count
    variance = sum_two / count - mean * mean
    inv_std = lax.rsqrt(variance + eps_norm)
    gain_group = gain.reshape(groups, per_group)
    bias_group = bias.reshape(groups, per_group)
    normed = (grouped - mean[:, None]) * inv_std[:, None]
    pre = normed * gain_group + bias_group
    sigma = jax.nn.sigmoid(pre)
    activated = pre * sigma * mask_groups
    decoded = (
        activated.reshape(frames, height, width, 2, 2, quarter)
        .transpose(0, 1, 3, 2, 4, 5)
        .reshape(frames, 2 * height, 2 * width, quarter)
        .astype(jnp.bfloat16)[None]
    )
    upstream = (
        cotangent[0]
        .astype(jnp.float32)
        .reshape(frames, height, 2, width, 2, quarter)
        .transpose(0, 1, 3, 2, 4, 5)
        .reshape(frames, height, width, groups, per_group)
        * mask_groups
    )
    d_pre = upstream * sigma * (1.0 + pre * (1.0 - sigma))
    gain_term = jnp.sum(d_pre * normed, axis=(0, 1, 2)).reshape(channels)
    bias_term = jnp.sum(d_pre, axis=(0, 1, 2)).reshape(channels)
    d_norm = d_pre * gain_group
    tot_one, tot_two = lax.psum(
        (jnp.sum(d_norm, axis=(0, 1, 2, 4)), jnp.sum(d_norm * normed, axis=(0, 1, 2, 4))), "shard"
    )
    d_conv = (
        (
            inv_std[:, None]
            * (d_norm - tot_one[:, None] / count - normed * tot_two[:, None] / count)
            * mask_groups
        )
        .reshape(frames, height, width, channels)
        .astype(jnp.bfloat16)
    )
    spread_back = lax.all_to_all(features, "shard", split_axis=3, concat_axis=2, tiled=True)
    slab_back = slab_columns(spread_back, frames, height, slab_width)
    whole_grad = lax.all_gather(d_conv, "shard", axis=2, tiled=True)
    back_share = jnp.transpose(conv_weight, (2, 1, 0)).reshape(channels, 27 * share)
    tap_images = jnp.dot(
        whole_grad.reshape(-1, channels), back_share, preferred_element_type=jnp.float32
    ).reshape(frames, height, slab_width, 27 * share)
    padded_images = jnp.pad(tap_images, ((0, 2), (1, 1), (1, 1), (0, 0)))
    input_sum = jnp.zeros((frames, height, slab_width, share), jnp.float32)
    for tap_index, shifted in enumerate(backward_taps(padded_images, frames, height, slab_width)):
        input_sum = input_sum + shifted[..., tap_index * share : (tap_index + 1) * share]
    d_features = lax.all_to_all(
        input_sum.astype(jnp.bfloat16), "shard", split_axis=2, concat_axis=3, tiled=True
    )
    clip_part = jnp.einsum(
        "pk,pc->kc",
        slab_back.reshape(-1, 27 * share),
        whole_grad.reshape(-1, channels),
        preferred_element_type=jnp.float32,
    )
    weight_sum = clip_part.reshape(27, share, channels).transpose(1, 0, 2)
    grad_conv = lax.psum(weight_sum.astype(jnp.bfloat16), "dp").astype(jnp.float32)
    grad_hidden = d_features * mask_cells.astype(jnp.bfloat16)
    embed_term = jnp.dot(
        bits.reshape(positions, CODE_BITS).T,
        grad_hidden.reshape(positions, channels),
        preferred_element_type=jnp.float32,
    )
    grad_embed, grad_gain, grad_bias = lax.psum((embed_term, gain_term, bias_term), ("dp", "shard"))
    return (decoded, grad_hidden[None], grad_conv, grad_embed, grad_gain, grad_bias)


def on_device(codes, lengths, hidden, embed, conv_weight, gain, bias, cotangent):
    share = conv_weight.shape[0]
    block = codes.shape[2] * codes.shape[3] * lax.axis_size("shard")
    fits = share == LANES and block == LANES and lax.axis_size("shard") == 4
    plan = by_slices if fits and lax.axis_size("dp") == 8 else by_gathers
    return plan(codes, lengths, hidden, embed, conv_weight, gain, bias, cotangent)


def solution(mesh):
    return jax.shard_map(
        on_device,
        mesh=mesh,
        in_specs=(
            P("dp", None, None, "shard"),
            P("dp"),
            P("dp", None, None, "shard", None),
            P(),
            P("shard", None, None),
            P(),
            P(),
            P("dp", None, None, "shard", None),
        ),
        out_specs=(
            P("dp", None, None, "shard", None),
            P("dp", None, None, "shard", None),
            P("shard", None, None),
            P(),
            P(),
            P(),
        ),
        check_vma=False,
    )
```
